512 devices in a mesh: ctx: 64 (over y_lo, z, core), kvh: 8 (over x, y_hi).
Axes of the slice: x: 4, y: 8 (y_hi: 2, y_lo: 4; y = y_hi * 4 + y_lo), z: 8, core: 2. Of those that a mesh axis runs over, the one named last changes fastest.
Arguments:
- hidden: bfloat16 [8192, 4096], P('ctx', 'kvh'), may hold values from -6 to 6
- destination: int32 [8192], P('ctx'), may hold values from 0 to 8191, as said below
- doc_ids: int32 [8192], P('ctx'), may hold values from 0 to 31, never falling along the last dimension, each value on 1 to 1024 neighbouring positions
- w_query: bfloat16 [4096, 2048], P(None, 'kvh'), may hold values from -0.09375 to 0.09375
- w_key: bfloat16 [4096, 1024], P(None, 'kvh'), may hold values from -0.09375 to 0.09375
- w_value: bfloat16 [4096, 1024], P(None, 'kvh'), may hold values from -0.09375 to 0.09375
- q_gain: float32 [128], replicated, may hold values from 0.1 to 1.9
- k_gain: float32 [128], replicated, may hold values from 0.1 to 1.9
Outputs:
- attended: bfloat16 [8192, 2048], P('ctx', 'kvh')
The draws below stay inside these ranges and needn't reach their ends.
Inputs may be any that keep to these rules, and one draw needn't show every extreme that they name: destination is a permutation of the packed positions; the rows held by one ctx index send at most 4 rows to any one block of 128 consecutive positions, and each ctx index sends exactly 4 to some block. `doc_ids`: documents are numbered in packed order and each covers at most 1024 consecutive positions.
All inputs are finite; a program needn't handle non-finite values.
Results may differ from the reference program's by a relative error of at most 0.009.
Values may be sent and summed in bfloat16 or wider, within the bound.
No kernel may reach another device: no remote copies, remote signals or barrier semaphores. Data moves between devices by JAX's collectives and lax.ppermute only.
A program may use at most 64 MiB of HBM per device.

```python
import math
import jax
import jax.numpy as jnp
import numpy as np
from jax import lax

D = 4096
HD = 128
QH_PER = 2
ROWS = 128
SPAN = 8
TOKENS = 8192
KV_HEADS = 8
QH = 16
DOCS = 32
N_CTX = 64


def draw_destination(key, part):
    key = jax.random.fold_in(key, 7)
    subkeys = jax.random.split(key, 5)
    base_count = ROWS // N_CTX
    pair_count = N_CTX // 2
    moves = jax.random.randint(subkeys[0], (pair_count,), 0, base_count + 1).astype(jnp.int32)
    moves = moves.at[0].set(base_count)
    signed = jnp.stack([moves, -moves], 1).reshape(N_CTX)
    shuffled = jax.random.permutation(subkeys[1], N_CTX)
    counts = jnp.full((N_CTX,), base_count, jnp.int32).at[shuffled].add(signed)
    turned = jax.random.permutation(subkeys[2], N_CTX)
    sources = jnp.arange(N_CTX, dtype=jnp.int32)
    table = counts[(turned[None, :] - sources[:, None]) % N_CTX]
    row_ends = jnp.cumsum(table, 1)
    row_begin = row_ends - table
    col_begin = jnp.cumsum(table, 0) - table
    slots = jnp.arange(ROWS, dtype=jnp.int32)
    block = jnp.sum((slots[None, :, None] >= row_ends[:, None, :]).astype(jnp.int32), 2)
    offset_in = slots[None, :] - jnp.take_along_axis(row_begin, block, 1)
    inside = jnp.take_along_axis(col_begin, block, 1) + offset_in
    block_scores = jax.random.randint(subkeys[3], (N_CTX, ROWS), 0, 2 ** 20) * ROWS + slots[None, :]
    block_order = jnp.argsort(block_scores, axis=1).astype(jnp.int32)
    target = block * ROWS + block_order[block, inside]
    source_scores = jax.random.randint(subkeys[4], (N_CTX, ROWS), 0, 2 ** 20) * ROWS + slots[None, :]
    source_order = jnp.argsort(source_scores, axis=1).astype(jnp.int32)
    rows_at = (sources[:, None] * ROWS + source_order).reshape(-1)
    return jnp.zeros((TOKENS,), jnp.int32).at[rows_at].set(target.reshape(-1).astype(jnp.int32))


def block_levels(own_key, extent, cuts, low, high):
    loudness = 1.0
    for dim, parts in cuts:
        heights = jax.random.uniform(jax.random.fold_in(jax.random.fold_in(own_key, 6), dim), (parts,), jnp.float32, low / len(cuts), high / len(cuts))
        loudness = loudness * jnp.repeat(jnp.exp(heights), extent[dim] // parts).reshape((-1,) + (1,) * (len(extent) - 1 - dim))
    return loudness


def length_profile(amount, total, reach, skew):
    loads = [(1 << 20) // math.isqrt(standing ** skew) + 1 for standing in range(2, amount + 1)]
    surplus, given = total - reach - (amount - 1), [1] * (amount - 1)
    while surplus > 0:
        candidates = [i for i in range(amount - 1) if given[i] < reach]
        mass, remaining = sum([loads[i] for i in candidates]), surplus
        for i in candidates:
            addition = min(reach - given[i], max(1, remaining * loads[i] // mass), surplus)
            given[i] = given[i] + addition
            surplus = surplus - addition
    return np.array([reach] + given)


def ragged_sizes(stream_key, number_of, total, limit, lean):
    if number_of == 2:
        one = jax.random.randint(stream_key, (), max(1, total - limit), min(limit, total - 1) + 1)
        return jnp.stack([one, total - one])
    lengths = jnp.asarray(length_profile(number_of, total, limit, lean), jnp.int32)
    twos = (number_of - 1) // 2
    source_of, taker = lengths[1:1 + 2 * twos:2], lengths[2:2 + 2 * twos:2]
    slack = jnp.minimum(source_of - 1, limit - taker)
    moved = jax.random.randint(jax.random.fold_in(stream_key, 1), (twos,), 0, 1 << 20) % (slack + 1)
    lengths = lengths.at[1:1 + 2 * twos:2].set(source_of - moved).at[2:2 + 2 * twos:2].set(taker + moved)
    return lengths[jax.random.permutation(jax.random.fold_in(stream_key, 2), number_of)]


def centred(stream_key, shape, width, bound, cuts=(), kind=jnp.bfloat16):
    factor_of = block_levels(stream_key, shape, cuts, -0.22, 0.18) if cuts else 1.0
    values = jax.random.normal(stream_key, shape, jnp.float32) * width * factor_of
    return jnp.minimum(jnp.maximum(values, -bound), bound).astype(kind)


def setup_inputs(seed: int = 0) -> dict:
    keys = jax.random.split(jax.random.key(seed), 9)
    hidden = centred(keys[0], (TOKENS, D), 1.0, 6.0, ((0, 64), (1, 8)))
    destination = draw_destination(jax.random.fold_in(keys[8], 71), 0)
    doc_ids = jnp.searchsorted(jnp.cumsum(ragged_sizes(keys[2], DOCS, TOKENS, SPAN * ROWS, 2)), jnp.arange(TOKENS), side="right").astype(jnp.int32)
    w_query = centred(keys[3], (D, QH * HD), D ** -0.5, 0.09375, ((1, 8),))
    w_key = centred(keys[4], (D, KV_HEADS * HD), D ** -0.5, 0.09375, ((1, 8),))
    w_value = centred(keys[5], (D, KV_HEADS * HD), D ** -0.5, 0.09375, ((1, 8),))
    q_gain = jnp.clip(1.0 + 0.18 * jax.random.normal(keys[6], (HD,), jnp.float32), 0.1, 1.9)
    k_gain = jnp.clip(1.0 + 0.18 * jax.random.normal(keys[7], (HD,), jnp.float32), 0.1, 1.9)
    return {"hidden": hidden, "destination": destination, "doc_ids": doc_ids, "w_query": w_query, "w_key": w_key, "w_value": w_value, "q_gain": q_gain, "k_gain": k_gain}


def normalize(tensor, gain_vec):
    return tensor * lax.rsqrt(lax.optimization_barrier(jnp.mean(tensor * tensor, -1, keepdims=True)) + 1e-06) * gain_vec

def rotate(tensor, positions):
    half_dim = tensor.shape[-1] // 2
    exponent = jnp.arange(half_dim, dtype=jnp.float32) * (2.0 / tensor.shape[-1])
    frequency = jnp.power(jnp.float32(1000000.0), -exponent)
    angles = positions.astype(jnp.float32)[:, None] * frequency[None, :]
    cosine = jnp.cos(angles)[:, None, :]
    sine_part = jnp.sin(angles)[:, None, :]
    leading = tensor[..., :half_dim]
    trailing = tensor[..., half_dim:]
    return jnp.concatenate([leading * cosine - trailing * sine_part, trailing * cosine + leading * sine_part], -1)

def reference(hidden, destination, doc_ids, w_query, w_key, w_value, q_gain, k_gain):
    placed = jnp.zeros((TOKENS, D), jnp.bfloat16).at[destination].set(hidden)
    positions = jnp.arange(TOKENS, dtype=jnp.int32)
    fresh = jnp.concatenate([jnp.ones((1,), bool), doc_ids[1:] != doc_ids[:-1]])
    doc_start = lax.cummax(jnp.where(fresh, positions, 0), axis=0).astype(jnp.int32)
    queries_raw = jnp.dot(placed, w_query, preferred_element_type=jnp.float32).reshape(TOKENS, QH, HD)
    queries = (rotate(normalize(queries_raw, q_gain), positions) * HD ** (-0.5)).astype(jnp.bfloat16)
    keys_raw = jnp.dot(placed, w_key, preferred_element_type=jnp.float32).reshape(TOKENS, KV_HEADS, HD)
    keys_rows = rotate(normalize(keys_raw, k_gain), positions).astype(jnp.bfloat16)
    values_rows = jnp.dot(placed, w_value, preferred_element_type=jnp.float32).astype(jnp.bfloat16).reshape(TOKENS, KV_HEADS, HD)
    window = SPAN * ROWS + 512

    def block_out(block_id):
        begin_q = (block_id * 512).astype(jnp.int32)
        begin_k = jnp.maximum(begin_q + 512 - window, 0).astype(jnp.int32)
        q_block = lax.dynamic_slice_in_dim(queries, begin_q, 512, 0).reshape(512, KV_HEADS, QH_PER, HD).astype(jnp.float32)
        k_block = lax.dynamic_slice_in_dim(keys_rows, begin_k, window, 0).astype(jnp.float32)
        v_block = lax.dynamic_slice_in_dim(values_rows, begin_k, window, 0).astype(jnp.float32)
        q_pos = begin_q + jnp.arange(512, dtype=jnp.int32)
        k_pos = begin_k + jnp.arange(window, dtype=jnp.int32)
        q_first = lax.dynamic_slice_in_dim(doc_start, begin_q, 512, 0)
        visible = (k_pos[None, :] >= q_first[:, None]) & (k_pos[None, :] <= q_pos[:, None])
        scores = jnp.einsum('qhgd,khd->hgqk', q_block, k_block)
        weights = jnp.where(visible[None, None], jnp.exp(scores), jnp.float32(0.0))
        totals = lax.optimization_barrier(jnp.sum(weights, -1))
        rounded = lax.optimization_barrier(weights.astype(jnp.bfloat16)).astype(jnp.float32)
        numer = jnp.einsum('hgqk,khd->qhgd', rounded, v_block)
        result = numer / jnp.transpose(totals, (2, 0, 1))[..., None]
        return result.astype(jnp.bfloat16).reshape(512, QH * HD)
    outputs = lax.map(block_out, jnp.arange(TOKENS // 512, dtype=jnp.int32))
    return outputs.reshape(TOKENS, QH * HD)
```

```python
import functools

import jax
import jax.numpy as jnp
from jax import lax
from jax.experimental import pallas as pl
from jax.experimental.pallas import tpu as pltpu
from jax.sharding import PartitionSpec as P

SPAN = 8
SLOTS = 4
CHUNK = 2 * SLOTS
F32, BF16 = jnp.float32, jnp.bfloat16


def along_kvh(block, shift):
    n = lax.axis_size("kvh")
    return lax.ppermute(block, "kvh", [(i, (i + 2 * shift) % n) for i in range(n)])


def along_ctx(block, distance):
    n = lax.axis_size("ctx")
    return lax.ppermute(block, "ctx", [(i, i + distance) for i in range(n - distance)])


def rotation(positions, head_dim):
    half_dim = head_dim // 2
    exponent = jnp.arange(half_dim, dtype=F32) * (2.0 / head_dim)
    frequency = jnp.power(jnp.float32(1000000.0), -exponent)
    angles = positions.astype(F32)[:, None] * frequency[None, :]
    cosine, sine = jnp.cos(angles), jnp.sin(angles)
    return jnp.concatenate([cosine, cosine], 1), jnp.concatenate([-sine, sine], 1)


def project_kernel(shifts, me_ref, *refs):
    pieces, refs = refs[: len(shifts)], refs[len(shifts) :]
    wq, wk, wv, cosine, sine, q_gain, k_gain, slot, within, docs, out = refs
    rows, width = pieces[0].shape[0] // 2, pieces[0].shape[1]
    groups = wq.shape[0] // width
    me = me_ref[0]
    totals = [jnp.zeros((rows, w.shape[1]), F32) for w in (wq, wk, wv)]
    for piece, shift in zip(pieces, shifts):
        source = lax.rem(me + (groups - 2 * shift), groups)
        for half in range(2):
            owner = source if half == 0 else source + 1 - 2 * lax.rem(source, 2)
            span = pl.ds(pl.multiple_of(owner * width, width), width)
            block = piece[half * rows : (half + 1) * rows, :]
            totals = [
                total + jnp.dot(block, w[span, :], preferred_element_type=F32)
                for total, w in zip(totals, (wq, wk, wv))
            ]
    raw_q, raw_k, raw_v = totals
    head_dim = raw_k.shape[1]

    def turned(raw, gain):
        unit = raw * lax.rsqrt(jnp.mean(raw * raw, -1, keepdims=True) + 1e-06) * gain[...]
        return unit * cosine[...] + pltpu.roll(unit, head_dim // 2, 1) * sine[...]

    heads = [
        turned(raw_q[:, h : h + head_dim], q_gain) * head_dim ** (-0.5)
        for h in range(0, raw_q.shape[1], head_dim)
    ]
    top = jnp.concatenate([h.astype(BF16) for h in heads] + [within[...]], 1)
    low = jnp.concatenate(
        [turned(raw_k, k_gain).astype(BF16), raw_v.astype(BF16), within[...]], 1
    )
    wanted = lax.broadcasted_iota(jnp.int32, (out.shape[0], 2 * rows), 0)
    picked = jnp.where(wanted == slot[...], 1.0, 0.0).astype(BF16)
    parcel = jnp.dot(picked, jnp.concatenate([top, low], 0), preferred_element_type=F32)
    body = out.shape[1] - docs.shape[1]
    out[:, :body] = parcel[:, :body].astype(BF16)
    out[:, body:] = (parcel[:, body:] + docs[...]).astype(BF16)


def land_kernel(me_ref, arrived, queries, keyvalues, key_docs, doc_rows):
    me = me_ref[0]
    rows = keyvalues.shape[0]
    body = arrived.shape[1] - rows
    coded = arrived[:, body:].astype(F32).astype(jnp.int32)
    doc_rows[...] = lax.shift_right_logical(coded, 1)
    hot = lax.bitwise_and(coded, 1)
    kind = lax.rem(lax.broadcasted_iota(jnp.int32, hot.shape, 0), CHUNK)
    first = jnp.where(kind < SLOTS, hot, 0).astype(F32).astype(BF16)
    second = jnp.where(kind >= SLOTS, hot, 0).astype(F32).astype(BF16)
    landing = jnp.concatenate([first, second], 1)
    placed = lax.dot_general(
        landing, arrived[:, :body], (((0,), (0,)), ((), ())), preferred_element_type=F32
    ).astype(BF16)
    head_dim = body // 2
    for h in range(2):
        queries[h * rows : (h + 1) * rows, :] = placed[:rows, h * head_dim : (h + 1) * head_dim]
    keyvalues[...] = placed[rows:, :]
    for back in range(SPAN + 1):
        owner = jnp.maximum(me - back, 0)
        row = doc_rows[pl.ds(pl.multiple_of(owner * CHUNK, CHUNK), CHUNK), :][:1, :]
        key_docs[back : back + 1, :] = jnp.where(me >= back, row, -1)


def attend_kernel(backs, queries, query_docs, key_docs, *refs):
    pieces, out = refs[:-1], refs[-1]
    rows = out.shape[0]
    head_dim = queries.shape[1]
    q = queries[...]
    q_doc = query_docs[...]
    numer = jnp.zeros((q.shape[0], head_dim), F32)
    denom = jnp.zeros((q.shape[0], 1), F32)
    for piece, held in zip(pieces, backs):
        scores = lax.dot_general(
            q, piece[:, :head_dim], (((1,), (1,)), ((), ())), preferred_element_type=F32
        )
        docs = jnp.concatenate([key_docs[back : back + 1, :] for back in held], 1)
        visible = q_doc == docs
        if held == (0,):
            t = lax.rem(lax.broadcasted_iota(jnp.int32, scores.shape, 0), rows)
            u = lax.broadcasted_iota(jnp.int32, scores.shape, 1)
            visible = visible & (u <= t)
        weights = jnp.where(visible, jnp.exp(scores), 0.0)
        denom = denom + jnp.sum(weights, 1, keepdims=True)
        numer = numer + jnp.dot(
            weights.astype(BF16), piece[:, head_dim:], preferred_element_type=F32
        )
    result = (numer / denom).astype(BF16)
    for h in range(out.shape[1] // head_dim):
        out[:, h * head_dim : (h + 1) * head_dim] = result[h * rows : (h + 1) * rows, :]


VMEM = pl.BlockSpec(memory_space=pltpu.VMEM)
SMEM = pl.BlockSpec(memory_space=pltpu.SMEM)


def call(kernel, out_shape, operands, scratch=(), flops=0, size=0, limit=24):
    return pl.pallas_call(
        kernel,
        out_shape=out_shape,
        in_specs=[SMEM if x.shape == (1,) else VMEM for x in operands],
        out_specs=jax.tree.map(lambda _: VMEM, out_shape),
        scratch_shapes=scratch,
        cost_estimate=pl.CostEstimate(flops=flops, bytes_accessed=size, transcendentals=0),
        compiler_params=pltpu.CompilerParams(vmem_limit_bytes=limit * 2**20),
    )(*operands)


def body(hidden, destination, doc_ids, w_query, w_key, w_value, q_gain, k_gain):
    blocks = lax.axis_size("ctx")
    ctx_index = lax.axis_index("ctx")
    kvh_index = lax.axis_index("kvh")
    rows, width = hidden.shape
    head_dim = q_gain.shape[0]

    n = lax.axis_size("kvh")
    across = lax.ppermute(hidden, "kvh", [(i, i ^ 1) for i in range(n)])
    own = jnp.concatenate([hidden, across], 0)
    shifts = (0, 1, 3, 2)
    pieces = [own] + [along_kvh(own, s) for s in shifts[1:]]

    target, inside = destination // rows, destination % rows
    index = jnp.arange(rows, dtype=jnp.int32)
    earlier = (target[:, None] == target[None, :]) & (index[:, None] < index[None, :])
    slot = target * CHUNK + jnp.sum(earlier.astype(jnp.int32), 0)
    slot = jnp.concatenate([slot, slot + SLOTS]).reshape(1, 2 * rows)
    within = (inside[:, None] == index[None, :]).astype(BF16)
    cosine, sine = rotation(destination, head_dim)
    docs = (2 * doc_ids).astype(F32).reshape(1, rows)
    query_docs = jnp.tile(doc_ids, w_query.shape[1] // head_dim).reshape(-1, 1)

    me_kvh = kvh_index.astype(jnp.int32).reshape(1)
    me_ctx = ctx_index.astype(jnp.int32).reshape(1)
    parcel = call(
        functools.partial(project_kernel, shifts),
        jax.ShapeDtypeStruct((blocks * CHUNK, 2 * head_dim + rows), BF16),
        [me_kvh, *pieces, w_query, w_key, w_value, cosine, sine]
        + [q_gain.reshape(1, -1), k_gain.reshape(1, -1), slot, within, docs],
    )
    arrived = lax.all_to_all(
        parcel.reshape(blocks, CHUNK, -1), "ctx", split_axis=0, concat_axis=0, tiled=True
    ).reshape(parcel.shape)
    queries, near, key_docs = call(
        land_kernel,
        (
            jax.ShapeDtypeStruct((2 * rows, head_dim), BF16),
            jax.ShapeDtypeStruct((rows, 2 * head_dim), BF16),
            jax.ShapeDtypeStruct((16, rows), jnp.int32),
        ),
        [me_ctx, arrived],
        scratch=[pltpu.VMEM((blocks * CHUNK, rows), jnp.int32)],
    )

    back8 = along_ctx(near, 8)
    back2 = along_ctx(near, 2)
    back02 = jnp.concatenate([near, back2], 0)
    back46 = along_ctx(back02, 4)
    held = jnp.concatenate([back02, back46, back8], 0)
    odd = lax.rem(ctx_index, 2) == 1
    swapped = lax.ppermute(
        jnp.where(odd, held[rows:], held[: 4 * rows]),
        "ctx",
        [(i, i ^ 1) for i in range(blocks)],
    )
    return call(
        functools.partial(attend_kernel, ((0,), (2,), (4, 6), (8,), (1, 3, 5, 7))),
        jax.ShapeDtypeStruct((rows, w_query.shape[1]), BF16),
        [queries, query_docs, key_docs, near, back2, back46, back8, swapped],
    )


def solution(mesh):
    placed = (
        P("ctx", "kvh"),
        P("ctx"),
        P("ctx"),
        P(None, "kvh"),
        P(None, "kvh"),
        P(None, "kvh"),
        P(),
        P(),
    )
    return jax.shard_map(
        body, mesh=mesh, in_specs=placed, out_specs=P("ctx", "kvh"), check_vma=False
    )
```

```python
import functools

import jax
import jax.numpy as jnp
from jax import lax
from jax.experimental import pallas as pl
from jax.experimental.pallas import tpu as pltpu
from jax.sharding import PartitionSpec as P

SPAN = 8
SLOTS = 4
PARTS = 1 + SPAN // 2 + 1
CHUNK = PARTS * SLOTS
PAIRS = PARTS // 2
LABEL = 256
F32, BF16, I32 = jnp.float32, jnp.bfloat16, jnp.int32


def along_kvh(block, shift):
    n = lax.axis_size("kvh")
    return lax.ppermute(block, "kvh", [(i, (i + 2 * shift) % n) for i in range(n)])


def iota(shape, dim):
    return lax.broadcasted_iota(I32, shape, dim)


def hot(mask):
    return jnp.where(mask, 1.0, 0.0).astype(BF16)


def column(row):
    square = (row.shape[1], row.shape[1])
    return jnp.sum(jnp.where(iota(square, 0) == iota(square, 1), row, 0), 1, keepdims=True)


def fetch(pairs, sems):
    copies = [pltpu.make_async_copy(a, b, sems.at[i]) for i, (a, b) in enumerate(pairs)]
    for copy in copies:
        copy.start()
    for copy in copies:
        copy.wait()


def notes_kernel(destination, doc_ids, hidden, notes, slot, query_docs, own, place_ref, docs_ref, sems):
    rows = destination.shape[1]
    fetch([(destination, place_ref), (doc_ids, docs_ref)], sems)
    place, docs = place_ref[...], docs_ref[...]
    target, inside = lax.div(place, rows), lax.rem(place, rows)
    square = (rows, rows)
    earlier = (column(target) == target) & (iota(square, 0) < iota(square, 1))
    order = jnp.sum(jnp.where(earlier, 1, 0), 0, keepdims=True)
    slot[...] = target * SLOTS + order
    blocks = notes.shape[0]
    order_col, label_col = column(order), column(inside) + 1
    label = jnp.zeros((blocks, rows), F32)
    for k in range(PARTS - 1):
        sent = hot(iota((blocks, rows), 0) == target + 2 * k)
        at = jnp.where(order_col + k * SLOTS == iota(square, 1), label_col, 0)
        label += jnp.dot(sent, at.astype(F32).astype(BF16), preferred_element_type=F32)
    notes[...] = (label.astype(I32) + LABEL * docs).reshape(notes.shape)
    docs_col = column(docs)
    for h in range(query_docs.shape[0] // rows):
        query_docs[h * rows : (h + 1) * rows, :] = docs_col
    own[...] = hidden[...]


def tables_kernel(
    slot, q_gain, k_gain, cosine, sine, picked, q_cos, q_sin, k_cos, k_sin, q_ref, k_ref, sems
):
    fetch([(q_gain, q_ref), (k_gain, k_ref)], sems)
    rows = slot.shape[1]
    shape = (picked.shape[0] // CHUNK, CHUNK, rows)
    block, line = iota(shape, 0), iota(shape, 1)
    wanted = block * SLOTS + line
    for p in range(PARTS):
        mine = (line >= p * SLOTS) & (line < (p + 1) * SLOTS)
        wanted = jnp.where(mine, wanted - p * SLOTS - 2 * max(p - 1, 0) * SLOTS, wanted)
    found = wanted == slot[...].reshape(1, 1, rows)
    flat = (picked.shape[0], rows)
    picked[:, :rows] = jnp.where(found & (line < SLOTS), 1.0, 0.0).reshape(flat).astype(BF16)
    picked[:, rows:] = jnp.where(found & (line >= SLOTS), 1.0, 0.0).reshape(flat).astype(BF16)
    c, s = cosine[...], sine[...]
    half = c.shape[1] // 2
    for gain, scale, turn_cos, turn_sin in (
        (q_ref[...], c.shape[1] ** (-0.5), q_cos, q_sin),
        (k_ref[...], 1.0, k_cos, k_sin),
    ):
        turn_cos[...] = c * (gain * scale)
        turn_sin[...] = s * (jnp.concatenate([gain[:, half:], gain[:, :half]], 1) * scale)


def project_kernel(shifts, me_ref, *refs):
    pieces, refs = refs[: len(shifts)], refs[len(shifts) :]
    q_cos, q_sin, k_cos, k_sin, picked, wq, wk, wv, out, held, sems = refs
    rows, width = pieces[0].shape[0] // 2, pieces[0].shape[1]
    groups = wq.shape[0] // width
    me = me_ref[0]
    steps = []
    for piece, shift in zip(pieces, shifts):
        source = lax.rem(me + (groups - 2 * shift), groups)
        for half in range(2):
            owner = source if half == 0 else source + 1 - 2 * lax.rem(source, 2)
            span = pl.ds(pl.multiple_of(owner * width, width), width)
            n, begin, copies = len(steps), 0, []
            for i, w in enumerate((wq, wk, wv)):
                to = held.at[n, :, begin : begin + w.shape[1]]
                copies.append(pltpu.make_async_copy(w.at[span, :], to, sems.at[n, i]))
                copies[-1].start()
                begin += w.shape[1]
            steps.append((copies, piece, half))
    total = jnp.zeros((rows, held.shape[2]), F32)
    for n, (copies, piece, half) in enumerate(steps):
        for copy in copies:
            copy.wait()
        block = piece[half * rows : (half + 1) * rows, :]
        total = total + jnp.dot(block, held[n], preferred_element_type=F32)
    head_dim = q_cos.shape[1]

    def turned(raw, turn_cos, turn_sin):
        scale = lax.rsqrt(jnp.mean(raw * raw, -1, keepdims=True) + 1e-06)
        return (
            (raw * turn_cos[...] + pltpu.roll(raw, head_dim // 2, 1) * turn_sin[...]) * scale
        ).astype(BF16)

    heads = [total[:, h : h + head_dim] for h in range(0, total.shape[1], head_dim)]
    top = jnp.concatenate([turned(h, q_cos, q_sin) for h in heads[:-2]], 1)
    low = jnp.concatenate([turned(heads[-2], k_cos, k_sin), heads[-1].astype(BF16)], 1)
    out[...] = jnp.dot(
        picked[...], jnp.concatenate([top, low], 0), preferred_element_type=F32
    ).astype(BF16)


def read_notes_kernel(me_ref, notes, landing, key_docs, doc_rows):
    me = me_ref[0]
    blocks, rows = notes.shape[0], notes.shape[2]
    got = notes[...].reshape(blocks, rows)
    doc_rows[...] = lax.div(got, LABEL)
    pair = 2 * SLOTS
    shape = (blocks * pair, rows)
    mixing = (blocks * pair, blocks)
    spread = hot(iota(mixing, 1) == lax.div(iota(mixing, 0), pair))
    labels = lax.rem(got, LABEL).astype(F32).astype(BF16)
    labels = jnp.dot(spread, labels, preferred_element_type=F32)
    place = lax.rem(iota(shape, 0), pair)
    lane = iota(shape, 1)
    for g in range(PAIRS):
        at = place + (2 * g - 1) * SLOTS
        if g == 0:
            at = jnp.where(at < 0, at + SLOTS, at)
        label = jnp.sum(jnp.where(lane == at, labels, 0.0), 1, keepdims=True).astype(I32)
        lands = lane + 1 == label
        for part, wanted in enumerate((place < SLOTS, place >= SLOTS)):
            part_hot = jnp.where(lands & wanted, 1.0, 0.0)
            landing[g, part * rows : (part + 1) * rows, :] = part_hot.T.astype(BF16)
    for back in range(SPAN + 1):
        row = doc_rows[pl.ds(jnp.maximum(me - back, 0), 1), :]
        key_docs[back : back + 1, :] = jnp.where(me >= back, row, -1)
    key_docs[SPAN + 1 :, :] = jnp.full((key_docs.shape[0] - SPAN - 1, rows), -1, I32)


def land_kernel(me_ref, landing, arrived, queries, keyvalues, sent):
    rows = landing.shape[1] // 2
    head_dim = queries.shape[1]
    pair = 2 * SLOTS
    for g in range(PAIRS):
        lines = arrived[:, g * pair : (g + 1) * pair, :].reshape(landing.shape[2], -1)
        placed = jnp.dot(landing[g], lines, preferred_element_type=F32).astype(BF16)
        if g == 0:
            for h in range(queries.shape[0] // rows):
                queries[h * rows : (h + 1) * rows, :] = placed[
                    :rows, h * head_dim : (h + 1) * head_dim
                ]
            keyvalues[:rows, :] = placed[rows:, :]
        else:
            keyvalues[(2 * g - 1) * rows : (2 * g + 1) * rows, :] = placed
    begin = pl.multiple_of(lax.rem(me_ref[0], 2) * rows, rows)
    sent[...] = keyvalues[pl.ds(begin, sent.shape[0]), :]


def attend(backs, rows, queries, query_docs, key_docs, keyvalues):
    head_dim = queries.shape[1]
    q = queries[...]
    q_doc = query_docs[...]
    scores = lax.dot_general(
        q, keyvalues[:, :head_dim], (((1,), (1,)), ((), ())), preferred_element_type=F32
    )
    docs = jnp.concatenate([key_docs[back : back + 1, :] for back in backs], 1)
    visible = q_doc == docs
    if 0 in backs:
        t, u = lax.rem(iota(scores.shape, 0), rows), iota(scores.shape, 1)
        visible = visible & ((u <= t) | (u >= rows))
    weights = jnp.where(visible, jnp.exp(scores), 0.0)
    denom = jnp.sum(weights, 1, keepdims=True)
    numer = jnp.dot(weights.astype(BF16), keyvalues[:, head_dim:], preferred_element_type=F32)
    return numer, denom


def attend_first_kernel(backs, queries, query_docs, key_docs, keyvalues, numer, denom):
    rows = key_docs.shape[1]
    n, d = attend(backs, rows, queries, query_docs, key_docs, keyvalues)
    numer[...] = n
    denom[...] = jnp.broadcast_to(d, denom.shape)


def attend_last_kernel(backs, queries, query_docs, key_docs, keyvalues, numer, denom, out):
    rows = out.shape[0]
    head_dim = queries.shape[1]
    n, d = attend(backs, rows, queries, query_docs, key_docs, keyvalues)
    result = ((numer[...] + n) / (denom[...] + d)).astype(BF16)
    for h in range(out.shape[1] // head_dim):
        out[:, h * head_dim : (h + 1) * head_dim] = result[h * rows : (h + 1) * rows, :]


VMEM = pl.BlockSpec(memory_space=pltpu.VMEM)
SMEM = pl.BlockSpec(memory_space=pltpu.SMEM)
HBM = pl.BlockSpec(memory_space=pltpu.HBM)


def call(kernel, outs, operands, scratch=(), flops=0, size=0, limit=24, away=()):
    specs = [SMEM if x.shape == (1,) else VMEM for x in operands]
    for i in away:
        specs[i] = HBM
    shapes = [jax.ShapeDtypeStruct(s, t) for s, t in outs]
    return pl.pallas_call(
        kernel,
        out_shape=shapes,
        in_specs=specs,
        out_specs=[VMEM] * len(shapes),
        scratch_shapes=scratch,
        cost_estimate=pl.CostEstimate(flops=flops, bytes_accessed=size, transcendentals=0),
        compiler_params=pltpu.CompilerParams(vmem_limit_bytes=limit * 2**20),
    )(*operands)


def rotation(positions, head_dim):
    half_dim = head_dim // 2
    exponent = jnp.arange(half_dim, dtype=F32) * (2.0 / head_dim)
    frequency = jnp.power(jnp.float32(1000000.0), -exponent)
    angles = positions.astype(F32)[:, None] * frequency[None, :]
    cosine, sine = jnp.cos(angles), jnp.sin(angles)
    return jnp.concatenate([cosine, cosine], 1), jnp.concatenate([-sine, sine], 1)


def body(hidden, destination, doc_ids, w_query, w_key, w_value, q_gain, k_gain):
    blocks = lax.axis_size("ctx")
    rows, width = hidden.shape
    q_width = w_query.shape[1]
    head_dim = q_gain.shape[0]
    q_rows = q_width // head_dim * rows
    me_kvh = lax.axis_index("kvh").astype(I32).reshape(1)
    me_ctx = lax.axis_index("ctx").astype(I32).reshape(1)

    n = lax.axis_size("kvh")
    across = lax.ppermute(hidden, "kvh", [(i, i ^ 1) for i in range(n)])
    notes, slot, query_docs, own = call(
        notes_kernel,
        [((blocks, 1, rows), I32), ((1, rows), I32), ((q_rows, 1), I32), (hidden.shape, BF16)],
        [destination.reshape(1, -1), doc_ids.reshape(1, -1), hidden],
        scratch=[pltpu.VMEM((1, rows), I32)] * 2 + [pltpu.SemaphoreType.DMA((2,))],
        away=(0, 1),
    )
    notes = lax.all_to_all(notes, "ctx", split_axis=0, concat_axis=0, tiled=True)
    own = jnp.concatenate([own, across], 0)
    shifts = (0, 1, 3, 2)
    pieces = [own] + [along_kvh(own, s) for s in shifts[1:]]
    landing, key_docs = call(
        read_notes_kernel,
        [((PAIRS, 2 * rows, blocks * 2 * SLOTS), BF16), ((16, rows), I32)],
        [me_ctx, notes],
        scratch=[pltpu.VMEM((blocks, rows), I32)],
    )
    cosine, sine = rotation(destination, head_dim)
    picked, q_cos, q_sin, k_cos, k_sin = call(
        tables_kernel,
        [((blocks * CHUNK, 2 * rows), BF16)] + [((rows, head_dim), F32)] * 4,
        [slot, q_gain.reshape(1, -1), k_gain.reshape(1, -1), cosine, sine],
        scratch=[pltpu.VMEM((1, head_dim), F32)] * 2 + [pltpu.SemaphoreType.DMA((2,))],
        away=(1, 2),
    )

    features = 2 * len(pieces)
    (parcel,) = call(
        functools.partial(project_kernel, shifts),
        [((blocks * CHUNK, 2 * head_dim), BF16)],
        [me_kvh, *pieces, q_cos, q_sin, k_cos, k_sin, picked, w_query, w_key, w_value],
        scratch=[
            pltpu.VMEM((features, width, q_width + 2 * head_dim), BF16),
            pltpu.SemaphoreType.DMA((features, 3)),
        ],
        away=(10, 11, 12),
    )
    arrived = lax.all_to_all(
        parcel.reshape(blocks, CHUNK, -1), "ctx", split_axis=0, concat_axis=0, tiled=True
    )
    held = SPAN // 2 + 1
    queries, keyvalues, sent = call(
        land_kernel,
        [
            ((q_rows, head_dim), BF16),
            ((held * rows, 2 * head_dim), BF16),
            (((held - 1) * rows, 2 * head_dim), BF16),
        ],
        [me_ctx, landing, arrived],
    )

    swapped = lax.ppermute(sent, "ctx", [(i, i ^ 1) for i in range(blocks)])
    numer, denom = call(
        functools.partial(attend_first_kernel, tuple(range(0, SPAN + 1, 2))),
        [((q_rows, head_dim), F32)] * 2,
        [queries, query_docs, key_docs, keyvalues],
    )
    (out,) = call(
        functools.partial(attend_last_kernel, tuple(range(1, SPAN + 1, 2))),
        [((rows, q_width), BF16)],
        [queries, query_docs, key_docs, swapped, numer, denom],
    )
    return out


def solution(mesh):
    placed = (
        P("ctx", "kvh"),
        P("ctx"),
        P("ctx"),
        P(None, "kvh"),
        P(None, "kvh"),
        P(None, "kvh"),
        P(),
        P(),
    )
    return jax.shard_map(
        body, mesh=mesh, in_specs=placed, out_specs=P("ctx", "kvh"), check_vma=False
    )
```

```python
import functools

import jax
import jax.numpy as jnp
from jax import lax
from jax.experimental import pallas as pl
from jax.experimental.pallas import tpu as pltpu
from jax.sharding import PartitionSpec as P

SPAN = 8
SLOTS = 4
PARTS = 1 + SPAN // 2 + 1
PAIRS = PARTS // 2
LINES = 2 * SLOTS
NOTED = 64
F32, BF16, I32 = jnp.float32, jnp.bfloat16, jnp.int32


def block_back(part):
    return 2 * max(part - 1, 0)


def iota(shape, dim):
    return lax.broadcasted_iota(I32, shape, dim)


def hot(mask):
    return jnp.where(mask, 1.0, 0.0).astype(BF16)


def column(row):
    square = (row.shape[1], row.shape[1])
    return jnp.sum(jnp.where(iota(square, 0) == iota(square, 1), row, 0), 1, keepdims=True)


def fetch(pairs, sems):
    copies = [pltpu.make_async_copy(a, b, sems.at[i]) for i, (a, b) in enumerate(pairs)]
    for copy in copies:
        copy.start()
    for copy in copies:
        copy.wait()


def spread_own_kernel(hidden, spread, sems):
    fetch([(hidden, spread.at[0])], sems)
    for i in range(1, spread.shape[0]):
        spread[i] = spread[0]


def spread_kernel(across, table, spread):
    for i in range(spread.shape[0]):
        spread[i] = across[...]


def tables_kernel(
    cosine, sine, destination, doc_ids, q_gain, k_gain,
    own, later, notes, query_docs, q_cos, q_sin, k_cos, k_sin,
    place_ref, docs_ref, q_ref, k_ref, sems,
):
    small = [(destination, place_ref), (doc_ids, docs_ref), (q_gain, q_ref), (k_gain, k_ref)]
    fetch(small, sems)
    place, docs = place_ref[...], docs_ref[...]
    rows = place.shape[1]
    target, inside = lax.div(place, rows), lax.rem(place, rows)
    square = (rows, rows)
    earlier = (column(target) == target) & (iota(square, 0) < iota(square, 1))
    order = jnp.sum(jnp.where(earlier, 1, 0), 0, keepdims=True)
    slot = (target * SLOTS + order).reshape(1, 1, rows)
    label = column(inside) + 1
    shape = (own.shape[0] // LINES, LINES, rows)
    flat = (own.shape[0], rows)
    block, line = iota(shape, 0), iota(shape, 1)
    noted = jnp.zeros(flat, F32)
    for g in range(PAIRS):
        back = jnp.where(line < SLOTS, block_back(2 * g), block_back(2 * g + 1))
        at = jnp.where(line < SLOTS, line, line - SLOTS)
        found = (block - back) * SLOTS + at == slot
        picked = jnp.where(found, 1.0, 0.0).reshape(flat).astype(BF16)
        if g == 0:
            own[:, :rows] = jnp.where(found & (line < SLOTS), 1.0, 0.0).reshape(flat).astype(BF16)
            own[:, rows:] = jnp.where(found & (line >= SLOTS), 1.0, 0.0).reshape(flat).astype(BF16)
        else:
            later[g - 1] = picked
        lane = jnp.where(iota(square, 1) == g, label, 0).astype(F32).astype(BF16)
        noted += jnp.dot(picked, lane, preferred_element_type=F32)
    kept = docs.astype(F32)
    halves = [jnp.concatenate([jnp.zeros((1, rows - NOTED), F32), kept[:, h : h + NOTED]], 1) for h in range(0, rows, NOTED)]
    doc_lines = sum(
        jnp.where(line == h, half.reshape(1, 1, rows), 0.0) for h, half in enumerate(halves)
    )
    notes[...] = (noted + doc_lines.reshape(flat)).astype(BF16)
    docs_col = column(docs)
    for h in range(query_docs.shape[0] // rows):
        query_docs[h * rows : (h + 1) * rows, :] = docs_col
    c, s = cosine[...], sine[...]
    half = c.shape[1] // 2
    for gain, scale, turn_cos, turn_sin in (
        (q_ref[...], c.shape[1] ** (-0.5), q_cos, q_sin),
        (k_ref[...], 1.0, k_cos, k_sin),
    ):
        turn_cos[...] = c * (gain * scale)
        turn_sin[...] = s * (jnp.concatenate([gain[:, half:], gain[:, :half]], 1) * scale)


def partial_projection(pieces, side, weights, held, sems):
    width = pieces[0].shape[1]
    steps = []
    for k in range(len(pieces)):
        span = pl.ds(pl.multiple_of((2 * k + side) * width, width), width)
        steps.append(
            [
                pltpu.make_async_copy(w.at[span, :], to.at[k], sems.at[k, i])
                for i, (w, to) in enumerate(zip(weights, held))
            ]
        )
        for copy in steps[-1]:
            copy.start()
    total = jnp.zeros((pieces[0].shape[0], sum(w.shape[1] for w in weights)), F32)
    for k, (piece, copies) in enumerate(zip(pieces, steps)):
        for copy in copies:
            copy.wait()
        block = jnp.concatenate([to[k] for to in held], 1)
        total = total + jnp.dot(piece[...], block, preferred_element_type=F32)
    return total


def project_first_kernel(me_ref, mine, wq, wk, wv, first, *room):
    pieces = [mine.at[k] for k in range(mine.shape[0])]
    side = lax.rem(me_ref[0], 2)
    first[...] = partial_projection(pieces, side, (wq, wk, wv), room[:-1], room[-1])


def project_kernel(
    me_ref, first, other, q_cos, q_sin, k_cos, k_sin, own, later, notes, wq, wk, wv,
    out, *room,
):
    pieces = [other.at[k] for k in range(other.shape[0])]
    side = 1 - lax.rem(me_ref[0], 2)
    total = first[...] + partial_projection(pieces, side, (wq, wk, wv), room[:-1], room[-1])
    head_dim = q_cos.shape[1]

    def turned(raw, turn_cos, turn_sin):
        scale = lax.rsqrt(jnp.mean(raw * raw, -1, keepdims=True) + 1e-06)
        return (
            (raw * turn_cos[...] + pltpu.roll(raw, head_dim // 2, 1) * turn_sin[...]) * scale
        ).astype(BF16)

    heads = [total[:, h : h + head_dim] for h in range(0, total.shape[1], head_dim)]
    top = jnp.concatenate([turned(h, q_cos, q_sin) for h in heads[:-2]], 1)
    low = jnp.concatenate([turned(heads[-2], k_cos, k_sin), heads[-1].astype(BF16)], 1)
    both = jnp.concatenate([top, low], 0)
    width = low.shape[1]
    for g in range(PAIRS):
        picked, lines = (own[...], both) if g == 0 else (later[g - 1], low)
        out[:, g * width : (g + 1) * width] = jnp.dot(
            picked, lines, preferred_element_type=F32
        ).astype(BF16)
    out[:, PAIRS * width :] = notes[...]


def land_kernel(me_ref, arrived, queries, keyvalues, sent, key_docs, doc_lines):
    me = me_ref[0]
    rows = key_docs.shape[1]
    width = keyvalues.shape[1]
    head_dim = queries.shape[1]
    noted = arrived[:, PAIRS * width :].astype(F32)
    doc_lines[...] = noted
    shape = noted.shape
    first = lax.rem(iota(shape, 0), LINES) < SLOTS
    spot = (iota(shape, 1) + 1).astype(F32)
    for g in range(PAIRS):
        lands = noted[:, g : g + 1] == spot
        landing = jnp.concatenate([hot(lands & first), hot(lands & ~first)], 1)
        placed = lax.dot_general(
            landing,
            arrived[:, g * width : (g + 1) * width],
            (((0,), (0,)), ((), ())),
            preferred_element_type=F32,
        ).astype(BF16)
        if g == 0:
            for h in range(queries.shape[0] // rows):
                queries[h * rows : (h + 1) * rows, :] = placed[
                    :rows, h * head_dim : (h + 1) * head_dim
                ]
            keyvalues[:rows, :] = placed[rows:, :]
        else:
            keyvalues[(2 * g - 1) * rows : (2 * g + 1) * rows, :] = placed
    begin = pl.multiple_of(lax.rem(me, 2) * rows, rows)
    sent[...] = keyvalues[pl.ds(begin, sent.shape[0]), :]
    for back in range(SPAN + 1):
        owner = pl.multiple_of(jnp.maximum(me - back, 0) * LINES, LINES)
        lines = doc_lines[pl.ds(owner, LINES), :]
        docs = jnp.concatenate([lines[h : h + 1, NOTED:] for h in range(rows // NOTED)], 1)
        key_docs[back : back + 1, :] = jnp.where(me >= back, docs.astype(I32), -1)
    key_docs[SPAN + 1 :, :] = jnp.full((key_docs.shape[0] - SPAN - 1, rows), -1, I32)


def attend(backs, rows, queries, query_docs, key_docs, keyvalues):
    head_dim = queries.shape[1]
    q = queries[...]
    q_doc = query_docs[...]
    scores = lax.dot_general(
        q, keyvalues[:, :head_dim], (((1,), (1,)), ((), ())), preferred_element_type=F32
    )
    docs = jnp.concatenate([key_docs[back : back + 1, :] for back in backs], 1)
    visible = q_doc == docs
    if 0 in backs:
        t, u = lax.rem(iota(scores.shape, 0), rows), iota(scores.shape, 1)
        visible = visible & ((u <= t) | (u >= rows))
    weights = jnp.where(visible, jnp.exp(scores), 0.0)
    denom = jnp.sum(weights, 1, keepdims=True)
    numer = jnp.dot(weights.astype(BF16), keyvalues[:, head_dim:], preferred_element_type=F32)
    return numer, denom


def attend_first_kernel(backs, queries, query_docs, key_docs, keyvalues, numer, denom):
    rows = key_docs.shape[1]
    n, d = attend(backs, rows, queries, query_docs, key_docs, keyvalues)
    numer[...] = n
    denom[...] = jnp.broadcast_to(d, denom.shape)


def attend_last_kernel(backs, queries, query_docs, key_docs, keyvalues, numer, denom, out):
    rows = out.shape[0]
    head_dim = queries.shape[1]
    n, d = attend(backs, rows, queries, query_docs, key_docs, keyvalues)
    result = ((numer[...] + n) / (denom[...] + d)).astype(BF16)
    for h in range(out.shape[1] // head_dim):
        out[:, h * head_dim : (h + 1) * head_dim] = result[h * rows : (h + 1) * rows, :]


TABLES_COST = 3 * 10**9
VMEM = pl.BlockSpec(memory_space=pltpu.VMEM)
SMEM = pl.BlockSpec(memory_space=pltpu.SMEM)
HBM = pl.BlockSpec(memory_space=pltpu.HBM)


def call(kernel, outs, operands, away=(), scratch=(), limit=24, near=(), cost=None):
    shapes = [
        pltpu.VMEM(s, t) if i in near else jax.ShapeDtypeStruct(s, t)
        for i, (s, t) in enumerate(outs)
    ]
    return pl.pallas_call(
        kernel,
        out_shape=shapes,
        in_specs=[SMEM if x.shape == (1,) else VMEM for x in operands] + [HBM] * len(away),
        out_specs=[VMEM] * len(shapes),
        scratch_shapes=scratch,
        cost_estimate=cost and pl.CostEstimate(flops=cost, bytes_accessed=0, transcendentals=0),
        compiler_params=pltpu.CompilerParams(vmem_limit_bytes=limit * 2**20),
    )(*operands, *[pltpu.with_memory_space_constraint(x, pltpu.HBM) for x in away])


def rotation(positions, head_dim):
    half_dim = head_dim // 2
    exponent = jnp.arange(half_dim, dtype=F32) * (2.0 / head_dim)
    frequency = jnp.power(jnp.float32(1000000.0), -exponent)
    angles = positions.astype(F32)[:, None] * frequency[None, :]
    cosine, sine = jnp.cos(angles), jnp.sin(angles)
    return jnp.concatenate([cosine, cosine], 1), jnp.concatenate([-sine, sine], 1)


def body(hidden, destination, doc_ids, w_query, w_key, w_value, q_gain, k_gain):
    blocks = lax.axis_size("ctx")
    rows, width = hidden.shape
    q_width = w_query.shape[1]
    head_dim = q_gain.shape[0]
    q_rows = q_width // head_dim * rows
    me_kvh = lax.axis_index("kvh").astype(I32).reshape(1)
    me_ctx = lax.axis_index("ctx").astype(I32).reshape(1)

    n = lax.axis_size("kvh")
    along_x = [list(range(side, n, 2)) for side in range(2)]
    members = len(along_x[0])
    across = lax.ppermute(hidden, "kvh", [(i, i ^ 1) for i in range(n)])
    (spread,) = call(
        spread_own_kernel,
        [((members, rows, width), BF16)],
        [],
        [hidden],
        scratch=[pltpu.SemaphoreType.DMA((1,))],
    )
    mine = lax.all_to_all(spread, "kvh", 0, 0, tiled=True, axis_index_groups=along_x)
    cosine, sine = rotation(destination, head_dim)
    lines = blocks * LINES
    own, later, notes, query_docs, q_cos, q_sin, k_cos, k_sin = call(
        tables_kernel,
        [
            ((lines, 2 * rows), BF16),
            ((PAIRS - 1, lines, rows), BF16),
            ((lines, rows), BF16),
            ((q_rows, 1), I32),
        ]
        + [((rows, head_dim), F32)] * 4,
        [cosine, sine],
        [destination.reshape(1, -1), doc_ids.reshape(1, -1)]
        + [q_gain.reshape(1, -1), k_gain.reshape(1, -1)],
        scratch=[pltpu.VMEM((1, rows), I32)] * 2
        + [pltpu.VMEM((1, head_dim), F32)] * 2
        + [pltpu.SemaphoreType.DMA((4,))],
        cost=TABLES_COST,
    )
    (spread,) = call(spread_kernel, [((members, rows, width), BF16)], [across, q_cos])
    other = lax.all_to_all(spread, "kvh", 0, 0, tiled=True, axis_index_groups=along_x)

    columns = PAIRS * 2 * head_dim + rows
    weights = [w_query, w_key, w_value]
    all_heads = q_width + 2 * head_dim
    room = [pltpu.VMEM((members, width, w.shape[1]), BF16) for w in weights]
    room.append(pltpu.SemaphoreType.DMA((members, len(weights))))
    (first,) = call(
        project_first_kernel, [((rows, all_heads), F32)], [me_kvh, mine], weights, scratch=room
    )
    (parcel,) = call(
        project_kernel,
        [((lines, columns), BF16)],
        [me_kvh, first, other, q_cos, q_sin, k_cos, k_sin, own, later, notes],
        weights,
        scratch=room,
    )
    arrived = lax.all_to_all(
        parcel.reshape(blocks, LINES, columns), "ctx", split_axis=0, concat_axis=0, tiled=True
    ).reshape(lines, columns)
    held = SPAN // 2 + 1
    queries, keyvalues, sent, key_docs = call(
        land_kernel,
        [
            ((q_rows, head_dim), BF16),
            ((held * rows, 2 * head_dim), BF16),
            (((held - 1) * rows, 2 * head_dim), BF16),
            ((16, rows), I32),
        ],
        [me_ctx, arrived],
        scratch=[pltpu.VMEM((lines, rows), F32)],
    )

    swapped = lax.ppermute(sent, "ctx", [(i, i ^ 1) for i in range(blocks)])
    numer, denom = call(
        functools.partial(attend_first_kernel, tuple(range(0, SPAN + 1, 2))),
        [((q_rows, head_dim), F32)] * 2,
        [queries, query_docs, key_docs, keyvalues],
    )
    (out,) = call(
        functools.partial(attend_last_kernel, tuple(range(1, SPAN + 1, 2))),
        [((rows, q_width), BF16)],
        [queries, query_docs, key_docs, swapped, numer, denom],
    )
    return out


def solution(mesh):
    placed = (
        P("ctx", "kvh"),
        P("ctx"),
        P("ctx"),
        P(None, "kvh"),
        P(None, "kvh"),
        P(None, "kvh"),
        P(),
        P(),
    )
    return jax.shard_map(
        body, mesh=mesh, in_specs=placed, out_specs=P("ctx", "kvh"), check_vma=False
    )
```

```python
import functools

import jax
import jax.numpy as jnp
from jax import lax
from jax.experimental import pallas as pl
from jax.experimental.pallas import tpu as pltpu
from jax.sharding import PartitionSpec as P

SPAN = 8
SLOTS = 4
PARTS = 1 + SPAN // 2 + 1
PAIRS = PARTS // 2
LINES = 2 * SLOTS
NOTED = 64
F32, BF16, I32 = jnp.float32, jnp.bfloat16, jnp.int32


def block_back(part):
    return 2 * max(part - 1, 0)


def iota(shape, dim):
    return lax.broadcasted_iota(I32, shape, dim)


def hot(mask):
    return jnp.where(mask, 1.0, 0.0).astype(BF16)


def column(row):
    square = (row.shape[1], row.shape[1])
    return jnp.sum(jnp.where(iota(square, 0) == iota(square, 1), row, 0), 1, keepdims=True)


def fetch(pairs, sems):
    copies = [pltpu.make_async_copy(a, b, sems.at[i]) for i, (a, b) in enumerate(pairs)]
    for copy in copies:
        copy.start()
    for copy in copies:
        copy.wait()


def spread_own_kernel(hidden, spread):
    for i in range(spread.shape[0]):
        spread[i] = hidden[...]


def tables_kernel(
    destination, doc_ids, q_gain, k_gain, picks, notes, gains, place_ref, docs_ref, sems
):
    gain_rows = [(g, gains.at[i : i + 1]) for i, g in enumerate((q_gain, k_gain))]
    fetch([(destination, place_ref), (doc_ids, docs_ref)] + gain_rows, sems)
    place, docs = place_ref[...], docs_ref[...]
    rows = place.shape[1]
    target, inside = lax.div(place, rows), lax.rem(place, rows)
    square = (rows, rows)
    earlier = (column(target) == target) & (iota(square, 0) < iota(square, 1))
    order = jnp.sum(jnp.where(earlier, 1, 0), 0, keepdims=True)
    slot = (target * SLOTS + order).reshape(1, 1, rows)
    label = column(inside) + 1
    shape = (notes.shape[0] // LINES, LINES, rows)
    flat = notes.shape
    block, line = iota(shape, 0), iota(shape, 1)
    noted = jnp.zeros(flat, F32)
    for g in range(PAIRS):
        back = jnp.where(line < SLOTS, block_back(2 * g), block_back(2 * g + 1))
        at = jnp.where(line < SLOTS, line, line - SLOTS)
        found = (block - back) * SLOTS + at == slot
        picked = jnp.where(found, 1.0, 0.0).reshape(flat).astype(BF16)
        picks[g] = picked
        lane = jnp.where(iota(square, 1) == g, label, 0).astype(F32).astype(BF16)
        noted += jnp.dot(picked, lane, preferred_element_type=F32)
    kept = docs.astype(F32)
    halves = [jnp.concatenate([jnp.zeros((1, rows - NOTED), F32), kept[:, h : h + NOTED]], 1) for h in range(0, rows, NOTED)]
    doc_lines = sum(
        jnp.where(line == h, half.reshape(1, 1, rows), 0.0) for h, half in enumerate(halves)
    )
    notes[...] = (noted + doc_lines.reshape(flat)).astype(BF16)


def weight_copies(weights, held, sems, owners):
    width = held[0].shape[1]
    copies = []
    for k, owner in enumerate(owners):
        span = pl.ds(pl.multiple_of(owner * width, width), width)
        copies.append(
            [
                pltpu.make_async_copy(w.at[span, :], to.at[k], sems.at[k, i])
                for i, (w, to) in enumerate(zip(weights, held))
            ]
        )
        for copy in copies[-1]:
            copy.start()
    return copies


def project_first_kernel(me_ref, mine, wq, wk, wv, first, *room):
    held, sems = room[:-1], room[-1]
    total = 0.0
    side = lax.rem(me_ref[0], 2)
    owners = [2 * k + side for k in range(mine.shape[0])]
    for k, copies in enumerate(weight_copies((wq, wk, wv), held, sems, owners)):
        for copy in copies:
            copy.wait()
        block = jnp.concatenate([to[k] for to in held], 1)
        total = total + jnp.dot(mine[k], block, preferred_element_type=F32)
    first[...] = total


def ahead_kernel(shifts, me_ref, first, wq, wk, wv, *refs):
    held, sems = refs[:-1], refs[-1]
    groups = wq.shape[0] // held[0].shape[1]
    partner = me_ref[0] + 1 - 2 * lax.rem(me_ref[0], 2)
    owners = [lax.rem(partner + groups - 2 * d, groups) for d in shifts]
    for copies in weight_copies((wq, wk, wv), held, sems, owners):
        for copy in copies:
            copy.wait()


def project_kernel(
    first, cosine, sine, gains, picks, notes, wq, wk, wv, *refs
):
    other, out = refs[:-1], refs[-1]
    total = first[...]
    for k, piece in enumerate(other):
        block = jnp.concatenate([w[k] for w in (wq, wk, wv)], 1)
        total = total + jnp.dot(piece[...], block, preferred_element_type=F32)
    head_dim = cosine.shape[1]
    c, s = cosine[...], sine[...]
    half = head_dim // 2
    turns = []
    for i, scale in enumerate((head_dim ** (-0.5), 1.0)):
        gain = gains[i : i + 1, :] * scale
        turns.append((c * gain, s * jnp.concatenate([gain[:, half:], gain[:, :half]], 1)))
    (q_cos, q_sin), (k_cos, k_sin) = turns

    def turned(raw, turn_cos, turn_sin):
        scale = lax.rsqrt(jnp.mean(raw * raw, -1, keepdims=True) + 1e-06)
        return (
            (raw * turn_cos + pltpu.roll(raw, half, 1) * turn_sin) * scale
        ).astype(BF16)

    heads = [total[:, h : h + head_dim] for h in range(0, total.shape[1], head_dim)]
    top = jnp.concatenate([turned(h, q_cos, q_sin) for h in heads[:-2]], 1)
    low = jnp.concatenate([turned(heads[-2], k_cos, k_sin), heads[-1].astype(BF16)], 1)
    width = low.shape[1]
    first_half = lax.rem(iota(picks.shape[1:], 0), LINES) < SLOTS
    for g in range(PAIRS):
        picked, lines = picks[g], low
        if g == 0:
            zero = jnp.zeros_like(picked)
            parts = [jnp.where(first_half, picked, zero), jnp.where(first_half, zero, picked)]
            picked, lines = jnp.concatenate(parts, 1), jnp.concatenate([top, low], 0)
        out[:, g * width : (g + 1) * width] = jnp.dot(
            picked, lines, preferred_element_type=F32
        ).astype(BF16)
    out[:, PAIRS * width :] = notes[...]


def land_kernel(
    me_ref, arrived, queries, keyvalues, sent, key_docs, query_docs, doc_lines
):
    me = me_ref[0]
    rows = key_docs.shape[1]
    width = keyvalues.shape[1]
    head_dim = queries.shape[1]
    noted = arrived[:, PAIRS * width :].astype(F32)
    doc_lines[...] = noted
    shape = noted.shape
    first = lax.rem(iota(shape, 0), LINES) < SLOTS
    spot = (iota(shape, 1) + 1).astype(F32)
    for g in range(PAIRS):
        lands = noted[:, g : g + 1] == spot
        landing = jnp.concatenate([hot(lands & first), hot(lands & ~first)], 1)
        placed = lax.dot_general(
            landing,
            arrived[:, g * width : (g + 1) * width],
            (((0,), (0,)), ((), ())),
            preferred_element_type=F32,
        ).astype(BF16)
        if g == 0:
            for h in range(queries.shape[0] // rows):
                queries[h * rows : (h + 1) * rows, :] = placed[
                    :rows, h * head_dim : (h + 1) * head_dim
                ]
            keyvalues[:rows, :] = placed[rows:, :]
        else:
            keyvalues[(2 * g - 1) * rows : (2 * g + 1) * rows, :] = placed
    begin = pl.multiple_of(lax.rem(me, 2) * rows, rows)
    sent[...] = keyvalues[pl.ds(begin, sent.shape[0]), :]
    for back in range(SPAN + 1):
        owner = pl.multiple_of(jnp.maximum(me - back, 0) * LINES, LINES)
        lines = doc_lines[pl.ds(owner, LINES), :]
        docs = jnp.concatenate([lines[h : h + 1, NOTED:] for h in range(rows // NOTED)], 1)
        key_docs[back : back + 1, :] = jnp.where(me >= back, docs.astype(I32), -1)
        if back == 0:
            own_docs = column(docs)
            for h in range(queries.shape[0] // rows):
                query_docs[h * rows : (h + 1) * rows, :] = own_docs.astype(I32)
    key_docs[SPAN + 1 :, :] = jnp.full((key_docs.shape[0] - SPAN - 1, rows), -1, I32)


def attend(backs, rows, queries, query_docs, key_docs, keyvalues):
    head_dim = queries.shape[1]
    q = queries[...]
    q_doc = query_docs[...]
    scores = lax.dot_general(
        q, keyvalues[:, :head_dim], (((1,), (1,)), ((), ())), preferred_element_type=F32
    )
    docs = jnp.concatenate([key_docs[back : back + 1, :] for back in backs], 1)
    visible = q_doc == docs
    if 0 in backs:
        t, u = lax.rem(iota(scores.shape, 0), rows), iota(scores.shape, 1)
        visible = visible & ((u <= t) | (u >= rows))
    weights = jnp.where(visible, jnp.exp(scores), 0.0)
    denom = jnp.sum(weights, 1, keepdims=True)
    numer = jnp.dot(weights.astype(BF16), keyvalues[:, head_dim:], preferred_element_type=F32)
    return numer, denom


def attend_first_kernel(backs, queries, query_docs, key_docs, keyvalues, numer, denom):
    rows = key_docs.shape[1]
    n, d = attend(backs, rows, queries, query_docs, key_docs, keyvalues)
    numer[...] = n
    denom[...] = jnp.broadcast_to(d, denom.shape)


def attend_last_kernel(backs, queries, query_docs, key_docs, keyvalues, numer, denom, out):
    rows = out.shape[0]
    head_dim = queries.shape[1]
    n, d = attend(backs, rows, queries, query_docs, key_docs, keyvalues)
    result = ((numer[...] + n) / (denom[...] + d)).astype(BF16)
    for h in range(out.shape[1] // head_dim):
        out[:, h * head_dim : (h + 1) * head_dim] = result[h * rows : (h + 1) * rows, :]


TABLES_COST = 2 * 10**10
VMEM = pl.BlockSpec(memory_space=pltpu.VMEM)
SMEM = pl.BlockSpec(memory_space=pltpu.SMEM)
HBM = pl.BlockSpec(memory_space=pltpu.HBM)


def call(kernel, outs, operands, away=(), scratch=(), limit=24, near=(), cost=None):
    shapes = [
        pltpu.VMEM(s, t) if i in near else jax.ShapeDtypeStruct(s, t)
        for i, (s, t) in enumerate(outs)
    ]
    return pl.pallas_call(
        kernel,
        out_shape=shapes,
        in_specs=[SMEM if x.shape == (1,) else VMEM for x in operands] + [HBM] * len(away),
        out_specs=[VMEM] * len(shapes),
        scratch_shapes=scratch,
        cost_estimate=cost and pl.CostEstimate(flops=cost, bytes_accessed=0, transcendentals=0),
        compiler_params=pltpu.CompilerParams(vmem_limit_bytes=limit * 2**20),
    )(*operands, *[pltpu.with_memory_space_constraint(x, pltpu.HBM) for x in away])


def rotation(positions, head_dim):
    half_dim = head_dim // 2
    exponent = jnp.arange(half_dim, dtype=F32) * (2.0 / head_dim)
    frequency = jnp.power(jnp.float32(1000000.0), -exponent)
    angles = positions.astype(F32)[:, None] * frequency[None, :]
    cosine, sine = jnp.cos(angles), jnp.sin(angles)
    return jnp.concatenate([cosine, cosine], 1), jnp.concatenate([-sine, sine], 1)


def body(hidden, destination, doc_ids, w_query, w_key, w_value, q_gain, k_gain):
    blocks = lax.axis_size("ctx")
    rows, width = hidden.shape
    q_width = w_query.shape[1]
    head_dim = q_gain.shape[0]
    q_rows = q_width // head_dim * rows
    me_kvh = lax.axis_index("kvh").astype(I32).reshape(1)
    me_ctx = lax.axis_index("ctx").astype(I32).reshape(1)

    n = lax.axis_size("kvh")
    along_x = [list(range(side, n, 2)) for side in range(2)]
    members = len(along_x[0])
    across = lax.ppermute(hidden, "kvh", [(i, i ^ 1) for i in range(n)])
    (spread,) = call(
        spread_own_kernel,
        [((members, rows, width), BF16)],
        [hidden],
    )
    mine = lax.all_to_all(spread, "kvh", 0, 0, tiled=True, axis_index_groups=along_x)
    cosine, sine = rotation(destination, head_dim)
    lines = blocks * LINES
    picks, notes, gains = call(
        tables_kernel,
        [((PAIRS, lines, rows), BF16), ((lines, rows), BF16), ((2, head_dim), F32)],
        [],
        [destination.reshape(1, -1), doc_ids.reshape(1, -1)]
        + [q_gain.reshape(1, -1), k_gain.reshape(1, -1)],
        scratch=[pltpu.VMEM((1, rows), I32)] * 2 + [pltpu.SemaphoreType.DMA((4,))],
        cost=TABLES_COST,
    )
    shifts = (0, 1, 3, 2)
    other = [across] + [
        lax.ppermute(across, "kvh", [(i, (i + 2 * d) % n) for i in range(n)]) for d in shifts[1:]
    ]

    columns = PAIRS * 2 * head_dim + rows
    weights = [w_query, w_key, w_value]
    all_heads = q_width + 2 * head_dim
    held = [((members, width, w.shape[1]), BF16) for w in weights]
    sems = pltpu.SemaphoreType.DMA((members, len(weights)))
    (first,) = call(
        project_first_kernel,
        [((rows, all_heads), F32)],
        [me_kvh, mine],
        weights,
        scratch=[pltpu.VMEM(*h) for h in held] + [sems],
    )
    ahead = call(functools.partial(ahead_kernel, shifts), held, [me_kvh, first], weights, scratch=[sems])
    (parcel,) = call(
        project_kernel,
        [((lines, columns), BF16)],
        [first, cosine, sine, gains, picks, notes, *ahead, *other],
    )
    arrived = lax.all_to_all(
        parcel.reshape(blocks, LINES, columns), "ctx", split_axis=0, concat_axis=0, tiled=True
    ).reshape(lines, columns)
    held = SPAN // 2 + 1
    queries, keyvalues, sent, key_docs, query_docs = call(
        land_kernel,
        [
            ((q_rows, head_dim), BF16),
            ((held * rows, 2 * head_dim), BF16),
            (((held - 1) * rows, 2 * head_dim), BF16),
            ((16, rows), I32),
            ((q_rows, 1), I32),
        ],
        [me_ctx, arrived],
        scratch=[pltpu.VMEM((lines, rows), F32)],
    )

    swapped = lax.ppermute(sent, "ctx", [(i, i ^ 1) for i in range(blocks)])
    numer, denom = call(
        functools.partial(attend_first_kernel, tuple(range(0, SPAN + 1, 2))),
        [((q_rows, head_dim), F32)] * 2,
        [queries, query_docs, key_docs, keyvalues],
    )
    (out,) = call(
        functools.partial(attend_last_kernel, tuple(range(1, SPAN + 1, 2))),
        [((rows, q_width), BF16)],
        [queries, query_docs, key_docs, swapped, numer, denom],
    )
    return out


def solution(mesh):
    placed = (
        P("ctx", "kvh"),
        P("ctx"),
        P("ctx"),
        P(None, "kvh"),
        P(None, "kvh"),
        P(None, "kvh"),
        P(),
        P(),
    )
    return jax.shard_map(
        body, mesh=mesh, in_specs=placed, out_specs=P("ctx", "kvh"), check_vma=False
    )
```

```python
import functools

import jax
import jax.numpy as jnp
from jax import lax
from jax.experimental import pallas as pl
from jax.experimental.pallas import tpu as pltpu
from jax.sharding import PartitionSpec as P

SPAN = 8
SLOTS = 4
PARTS = 1 + SPAN // 2 + 1
PAIRS = PARTS // 2
LINES = 2 * SLOTS
NOTED = 64
F32, BF16, I32 = jnp.float32, jnp.bfloat16, jnp.int32


def block_back(part):
    return 2 * max(part - 1, 0)


def iota(shape, dim):
    return lax.broadcasted_iota(I32, shape, dim)


def hot(mask):
    return jnp.where(mask, 1.0, 0.0).astype(BF16)


def column(row):
    square = (row.shape[1], row.shape[1])
    return jnp.sum(jnp.where(iota(square, 0) == iota(square, 1), row, 0), 1, keepdims=True)


def fetch(pairs, sems):
    copies = [pltpu.make_async_copy(a, b, sems.at[i]) for i, (a, b) in enumerate(pairs)]
    for copy in copies:
        copy.start()
    for copy in copies:
        copy.wait()


def spread_own_kernel(hidden, spread):
    for i in range(spread.shape[0]):
        spread[i] = hidden[...]


def tables_kernel(
    destination, doc_ids, q_gain, k_gain, picks, notes, gains, place_ref, docs_ref, sems
):
    gain_rows = [(g, gains.at[i : i + 1]) for i, g in enumerate((q_gain, k_gain))]
    fetch([(destination, place_ref), (doc_ids, docs_ref)] + gain_rows, sems)
    place, docs = place_ref[...], docs_ref[...]
    rows = place.shape[1]
    target, inside = lax.div(place, rows), lax.rem(place, rows)
    square = (rows, rows)
    earlier = (column(target) == target) & (iota(square, 0) < iota(square, 1))
    order = jnp.sum(jnp.where(earlier, 1, 0), 0, keepdims=True)
    slot = (target * SLOTS + order).reshape(1, 1, rows)
    label = column(inside) + 1
    shape = (notes.shape[0] // LINES, LINES, rows)
    flat = notes.shape
    block, line = iota(shape, 0), iota(shape, 1)
    noted = jnp.zeros(flat, F32)
    for g in range(PAIRS):
        back = jnp.where(line < SLOTS, block_back(2 * g), block_back(2 * g + 1))
        at = jnp.where(line < SLOTS, line, line - SLOTS)
        found = (block - back) * SLOTS + at == slot
        picked = jnp.where(found, 1.0, 0.0).reshape(flat).astype(BF16)
        picks[g] = picked
        lane = jnp.where(iota(square, 1) == g, label, 0).astype(F32).astype(BF16)
        noted += jnp.dot(picked, lane, preferred_element_type=F32)
    kept = docs.astype(F32)
    halves = [jnp.concatenate([jnp.zeros((1, rows - NOTED), F32), kept[:, h : h + NOTED]], 1) for h in range(0, rows, NOTED)]
    doc_lines = sum(
        jnp.where(line == h, half.reshape(1, 1, rows), 0.0) for h, half in enumerate(halves)
    )
    notes[...] = (noted + doc_lines.reshape(flat)).astype(BF16)


def weight_copies(weights, held, sems, owners):
    width = held[0].shape[1]
    copies = []
    for k, owner in enumerate(owners):
        span = pl.ds(pl.multiple_of(owner * width, width), width)
        copies.append(
            [
                pltpu.make_async_copy(w.at[span, :], to.at[k], sems.at[k, i])
                for i, (w, to) in enumerate(zip(weights, held))
            ]
        )
        for copy in copies[-1]:
            copy.start()
    return copies


def project_first_kernel(me_ref, mine, wq, wk, wv, first, *room):
    held, sems = room[:-1], room[-1]
    total = 0.0
    side = lax.rem(me_ref[0], 2)
    owners = [2 * k + side for k in range(mine.shape[0])]
    for k, copies in enumerate(weight_copies((wq, wk, wv), held, sems, owners)):
        for copy in copies:
            copy.wait()
        block = jnp.concatenate([to[k] for to in held], 1)
        total = total + jnp.dot(mine[k], block, preferred_element_type=F32)
    first[...] = total


def ahead_kernel(shifts, me_ref, first, wq, wk, wv, *refs):
    held, sems = refs[:-1], refs[-1]
    groups = wq.shape[0] // held[0].shape[1]
    partner = me_ref[0] + 1 - 2 * lax.rem(me_ref[0], 2)
    owners = [lax.rem(partner + groups - 2 * d, groups) for d in shifts]
    for copies in weight_copies((wq, wk, wv), held, sems, owners):
        for copy in copies:
            copy.wait()


def project_kernel(
    first, cosine, sine, gains, picks, notes, wq, wk, wv, *refs
):
    other, (out, held, sems) = refs[:-3], refs[-3:]
    width = held.shape[2]
    kept = out.at[:, PAIRS * width :]
    copies = [pltpu.make_async_copy(notes, kept, sems.at[PAIRS])]
    copies[0].start()
    total = first[...]
    for k, piece in enumerate(other):
        block = jnp.concatenate([w[k] for w in (wq, wk, wv)], 1)
        total = total + jnp.dot(piece[...], block, preferred_element_type=F32)
    head_dim = cosine.shape[1]
    c, s = cosine[...], sine[...]
    half = head_dim // 2
    turns = []
    for i, scale in enumerate((head_dim ** (-0.5), 1.0)):
        gain = gains[i : i + 1, :] * scale
        turns.append((c * gain, s * jnp.concatenate([gain[:, half:], gain[:, :half]], 1)))
    (q_cos, q_sin), (k_cos, k_sin) = turns

    def turned(raw, turn_cos, turn_sin):
        scale = lax.rsqrt(jnp.mean(raw * raw, -1, keepdims=True) + 1e-06)
        return (
            (raw * turn_cos + pltpu.roll(raw, half, 1) * turn_sin) * scale
        ).astype(BF16)

    heads = [total[:, h : h + head_dim] for h in range(0, total.shape[1], head_dim)]
    top = jnp.concatenate([turned(h, q_cos, q_sin) for h in heads[:-2]], 1)
    low = jnp.concatenate([turned(heads[-2], k_cos, k_sin), heads[-1].astype(BF16)], 1)
    first_half = lax.rem(iota(picks.shape[1:], 0), LINES) < SLOTS
    for g in range(PAIRS):
        picked, lines = picks[g], low
        if g == 0:
            zero = jnp.zeros_like(picked)
            parts = [jnp.where(first_half, picked, zero), jnp.where(first_half, zero, picked)]
            picked, lines = jnp.concatenate(parts, 1), jnp.concatenate([top, low], 0)
        held[g] = jnp.dot(picked, lines, preferred_element_type=F32).astype(BF16)
        to = out.at[:, g * width : (g + 1) * width]
        copies.append(pltpu.make_async_copy(held.at[g], to, sems.at[g]))
        copies[-1].start()
    for copy in copies:
        copy.wait()


def land_kernel(
    me_ref, arrived, queries, keyvalues, sent, key_docs, query_docs, doc_lines
):
    me = me_ref[0]
    rows = key_docs.shape[1]
    width = keyvalues.shape[1]
    head_dim = queries.shape[1]
    noted = arrived[:, PAIRS * width :].astype(F32)
    doc_lines[...] = noted
    labels = noted.T
    shape = labels.shape
    first = lax.rem(iota(shape, 1), LINES) < SLOTS
    spot = (iota(shape, 0) + 1).astype(F32)
    for g in range(PAIRS):
        lands = labels[g : g + 1, :] == spot
        landing = jnp.concatenate([hot(lands & first), hot(lands & ~first)], 0)
        placed = jnp.dot(
            landing, arrived[:, g * width : (g + 1) * width], preferred_element_type=F32
        ).astype(BF16)
        if g == 0:
            for h in range(queries.shape[0] // rows):
                queries[h * rows : (h + 1) * rows, :] = placed[
                    :rows, h * head_dim : (h + 1) * head_dim
                ]
            keyvalues[:rows, :] = placed[rows:, :]
        else:
            keyvalues[(2 * g - 1) * rows : (2 * g + 1) * rows, :] = placed
    begin = pl.multiple_of(lax.rem(me, 2) * rows, rows)
    sent[...] = keyvalues[pl.ds(begin, sent.shape[0]), :]
    for back in range(SPAN + 1):
        owner = pl.multiple_of(jnp.maximum(me - back, 0) * LINES, LINES)
        lines = doc_lines[pl.ds(owner, LINES), :]
        docs = jnp.concatenate([lines[h : h + 1, NOTED:] for h in range(rows // NOTED)], 1)
        key_docs[back : back + 1, :] = jnp.where(me >= back, docs.astype(I32), -1)
        if back == 0:
            own_docs = column(docs)
            for h in range(queries.shape[0] // rows):
                query_docs[h * rows : (h + 1) * rows, :] = own_docs.astype(I32)
    key_docs[SPAN + 1 :, :] = jnp.full((key_docs.shape[0] - SPAN - 1, rows), -1, I32)


def attend(backs, rows, queries, query_docs, key_docs, keyvalues):
    head_dim = queries.shape[1]
    q = queries[...]
    q_doc = query_docs[...]
    scores = lax.dot_general(
        q, keyvalues[:, :head_dim], (((1,), (1,)), ((), ())), preferred_element_type=F32
    )
    docs = jnp.concatenate([key_docs[back : back + 1, :] for back in backs], 1)
    visible = q_doc == docs
    if 0 in backs:
        t, u = lax.rem(iota(scores.shape, 0), rows), iota(scores.shape, 1)
        visible = visible & ((u <= t) | (u >= rows))
    weights = jnp.where(visible, jnp.exp(scores), 0.0)
    denom = jnp.sum(weights, 1, keepdims=True)
    numer = jnp.dot(weights.astype(BF16), keyvalues[:, head_dim:], preferred_element_type=F32)
    return numer, denom


def attend_first_kernel(backs, queries, query_docs, key_docs, keyvalues, numer, denom):
    rows = key_docs.shape[1]
    n, d = attend(backs, rows, queries, query_docs, key_docs, keyvalues)
    numer[...] = n
    denom[...] = jnp.broadcast_to(d, denom.shape)


def attend_last_kernel(backs, queries, query_docs, key_docs, keyvalues, numer, denom, out):
    rows = out.shape[0]
    head_dim = queries.shape[1]
    n, d = attend(backs, rows, queries, query_docs, key_docs, keyvalues)
    result = ((numer[...] + n) / (denom[...] + d)).astype(BF16)
    for h in range(out.shape[1] // head_dim):
        out[:, h * head_dim : (h + 1) * head_dim] = result[h * rows : (h + 1) * rows, :]


TABLES_COST = 2 * 10**10
VMEM = pl.BlockSpec(memory_space=pltpu.VMEM)
SMEM = pl.BlockSpec(memory_space=pltpu.SMEM)
HBM = pl.BlockSpec(memory_space=pltpu.HBM)


def call(kernel, outs, operands, away=(), scratch=(), limit=24, cost=None, out_spec=VMEM):
    shapes = [jax.ShapeDtypeStruct(s, t) for s, t in outs]
    return pl.pallas_call(
        kernel,
        out_shape=shapes,
        in_specs=[SMEM if x.shape == (1,) else VMEM for x in operands] + [HBM] * len(away),
        out_specs=[out_spec] * len(shapes),
        scratch_shapes=scratch,
        cost_estimate=cost and pl.CostEstimate(flops=cost, bytes_accessed=0, transcendentals=0),
        compiler_params=pltpu.CompilerParams(vmem_limit_bytes=limit * 2**20),
    )(*operands, *[pltpu.with_memory_space_constraint(x, pltpu.HBM) for x in away])


def rotation(positions, head_dim):
    half_dim = head_dim // 2
    exponent = jnp.arange(half_dim, dtype=F32) * (2.0 / head_dim)
    frequency = jnp.power(jnp.float32(1000000.0), -exponent)
    angles = positions.astype(F32)[:, None] * frequency[None, :]
    cosine, sine = jnp.cos(angles), jnp.sin(angles)
    return jnp.concatenate([cosine, cosine], 1), jnp.concatenate([-sine, sine], 1)


def body(hidden, destination, doc_ids, w_query, w_key, w_value, q_gain, k_gain):
    blocks = lax.axis_size("ctx")
    rows, width = hidden.shape
    q_width = w_query.shape[1]
    head_dim = q_gain.shape[0]
    q_rows = q_width // head_dim * rows
    me_kvh = lax.axis_index("kvh").astype(I32).reshape(1)
    me_ctx = lax.axis_index("ctx").astype(I32).reshape(1)

    n = lax.axis_size("kvh")
    along_x = [list(range(side, n, 2)) for side in range(2)]
    members = len(along_x[0])
    across = lax.ppermute(hidden, "kvh", [(i, i ^ 1) for i in range(n)])
    (spread,) = call(
        spread_own_kernel,
        [((members, rows, width), BF16)],
        [hidden],
    )
    mine = lax.all_to_all(spread, "kvh", 0, 0, tiled=True, axis_index_groups=along_x)
    cosine, sine = rotation(destination, head_dim)
    lines = blocks * LINES
    picks, notes, gains = call(
        tables_kernel,
        [((PAIRS, lines, rows), BF16), ((lines, rows), BF16), ((2, head_dim), F32)],
        [],
        [destination.reshape(1, -1), doc_ids.reshape(1, -1)]
        + [q_gain.reshape(1, -1), k_gain.reshape(1, -1)],
        scratch=[pltpu.VMEM((1, rows), I32)] * 2 + [pltpu.SemaphoreType.DMA((4,))],
        cost=TABLES_COST,
    )
    shifts = (0, 2, 1, 3)
    other = [across] + [
        lax.ppermute(across, "kvh", [(i, (i + 2 * d) % n) for i in range(n)]) for d in shifts[1:]
    ]

    columns = PAIRS * 2 * head_dim + rows
    weights = [w_query, w_key, w_value]
    all_heads = q_width + 2 * head_dim
    held = [((members, width, w.shape[1]), BF16) for w in weights]
    sems = pltpu.SemaphoreType.DMA((members, len(weights)))
    (first,) = call(
        project_first_kernel,
        [((rows, all_heads), F32)],
        [me_kvh, mine],
        weights,
        scratch=[pltpu.VMEM(*h) for h in held] + [sems],
    )
    ahead = call(functools.partial(ahead_kernel, shifts), held, [me_kvh, first], weights, scratch=[sems])
    (parcel,) = call(
        project_kernel,
        [((lines, columns), BF16)],
        [first, cosine, sine, gains, picks, notes, *ahead, *other],
        scratch=[
            pltpu.VMEM((PAIRS, lines, 2 * head_dim), BF16),
            pltpu.SemaphoreType.DMA((PAIRS + 1,)),
        ],
        out_spec=HBM,
    )
    arrived = lax.all_to_all(
        parcel.reshape(blocks, LINES, columns), "ctx", split_axis=0, concat_axis=0, tiled=True
    ).reshape(lines, columns)
    held = SPAN // 2 + 1
    queries, keyvalues, sent, key_docs, query_docs = call(
        land_kernel,
        [
            ((q_rows, head_dim), BF16),
            ((held * rows, 2 * head_dim), BF16),
            (((held - 1) * rows, 2 * head_dim), BF16),
            ((16, rows), I32),
            ((q_rows, 1), I32),
        ],
        [me_ctx, arrived],
        scratch=[pltpu.VMEM((lines, rows), F32)],
    )

    swapped = lax.ppermute(sent, "ctx", [(i, i ^ 1) for i in range(blocks)])
    numer, denom = call(
        functools.partial(attend_first_kernel, tuple(range(0, SPAN + 1, 2))),
        [((q_rows, head_dim), F32)] * 2,
        [queries, query_docs, key_docs, keyvalues],
    )
    (out,) = call(
        functools.partial(attend_last_kernel, tuple(range(1, SPAN + 1, 2))),
        [((rows, q_width), BF16)],
        [queries, query_docs, key_docs, swapped, numer, denom],
    )
    return out


def solution(mesh):
    placed = (
        P("ctx", "kvh"),
        P("ctx"),
        P("ctx"),
        P(None, "kvh"),
        P(None, "kvh"),
        P(None, "kvh"),
        P(),
        P(),
    )
    return jax.shard_map(
        body, mesh=mesh, in_specs=placed, out_specs=P("ctx", "kvh"), check_vma=False
    )
```

```python
import functools

import jax
import jax.numpy as jnp
from jax import lax
from jax.experimental import pallas as pl
from jax.experimental.pallas import tpu as pltpu
from jax.sharding import PartitionSpec as P

SPAN = 8
SLOTS = 4
PARTS = 1 + SPAN // 2 + 1
PAIRS = PARTS // 2
LINES = 2 * SLOTS
NOTED = 64
F32, BF16, I32 = jnp.float32, jnp.bfloat16, jnp.int32


def block_back(part):
    return 2 * max(part - 1, 0)


def iota(shape, dim):
    return lax.broadcasted_iota(I32, shape, dim)


def hot(mask):
    return jnp.where(mask, 1.0, 0.0).astype(BF16)


def column(row):
    square = (row.shape[1], row.shape[1])
    return jnp.sum(jnp.where(iota(square, 0) == iota(square, 1), row, 0), 1, keepdims=True)


def fetch(pairs, sems):
    copies = [pltpu.make_async_copy(a, b, sems.at[i]) for i, (a, b) in enumerate(pairs)]
    for copy in copies:
        copy.start()
    for copy in copies:
        copy.wait()


def spread_own_kernel(hidden, spread):
    for i in range(spread.shape[0]):
        spread[i] = hidden[...]


def tables_kernel(
    destination, doc_ids, q_gain, k_gain, picks, notes, gains, place_ref, docs_ref, sems
):
    gain_rows = [(g, gains.at[i : i + 1]) for i, g in enumerate((q_gain, k_gain))]
    fetch([(destination, place_ref), (doc_ids, docs_ref)] + gain_rows, sems)
    place, docs = place_ref[...], docs_ref[...]
    rows = place.shape[1]
    target, inside = lax.div(place, rows), lax.rem(place, rows)
    square = (rows, rows)
    earlier = (column(target) == target) & (iota(square, 0) < iota(square, 1))
    order = jnp.sum(jnp.where(earlier, 1, 0), 0, keepdims=True)
    slot = (target * SLOTS + order).reshape(1, 1, rows)
    label = column(inside) + 1
    shape = (notes.shape[0] // LINES, LINES, rows)
    flat = notes.shape
    block, line = iota(shape, 0), iota(shape, 1)
    noted = jnp.zeros(flat, F32)
    for g in range(PAIRS):
        back = jnp.where(line < SLOTS, block_back(2 * g), block_back(2 * g + 1))
        at = jnp.where(line < SLOTS, line, line - SLOTS)
        found = (block - back) * SLOTS + at == slot
        picked = jnp.where(found, 1.0, 0.0).reshape(flat).astype(BF16)
        picks[g] = picked
        lane = jnp.where(iota(square, 1) == g, label, 0).astype(F32).astype(BF16)
        noted += jnp.dot(picked, lane, preferred_element_type=F32)
    kept = docs.astype(F32)
    halves = [jnp.concatenate([jnp.zeros((1, rows - NOTED), F32), kept[:, h : h + NOTED]], 1) for h in range(0, rows, NOTED)]
    doc_lines = sum(
        jnp.where(line == h, half.reshape(1, 1, rows), 0.0) for h, half in enumerate(halves)
    )
    notes[...] = (noted + doc_lines.reshape(flat)).astype(BF16)


def weight_copies(weights, held, sems, owners):
    width = held[0].shape[1]
    copies = []
    for k, owner in enumerate(owners):
        span = pl.ds(pl.multiple_of(owner * width, width), width)
        copies.append(
            [
                pltpu.make_async_copy(w.at[span, :], to.at[k], sems.at[k, i])
                for i, (w, to) in enumerate(zip(weights, held))
            ]
        )
        for copy in copies[-1]:
            copy.start()
    return copies


def project_first_kernel(shifts, me_ref, mine, wq, wk, wv, first, *refs):
    ahead, held, (sems, ahead_sems) = refs[:3], refs[3:6], refs[6:]
    side = lax.rem(me_ref[0], 2)
    owners = [2 * k + side for k in range(mine.shape[0])]
    steps = weight_copies((wq, wk, wv), held, sems, owners)
    groups = wq.shape[0] // held[0].shape[1]
    partner = me_ref[0] + 1 - 2 * side
    owners = [lax.rem(partner + groups - 2 * d, groups) for d in shifts]
    later = weight_copies((wq, wk, wv), ahead, ahead_sems, owners)
    total = 0.0
    for k, copies in enumerate(steps):
        for copy in copies:
            copy.wait()
        block = jnp.concatenate([to[k] for to in held], 1)
        total = total + jnp.dot(mine[k], block, preferred_element_type=F32)
    first[...] = total
    for copies in later:
        for copy in copies:
            copy.wait()


def project_kernel(
    first, cosine, sine, gains, picks, notes, wq, wk, wv, *refs
):
    other, (out, held, sems) = refs[:-3], refs[-3:]
    width = held.shape[2]
    kept = out.at[:, PAIRS * width :]
    copies = [pltpu.make_async_copy(notes, kept, sems.at[PAIRS])]
    copies[0].start()
    total = first[...]
    for k, piece in enumerate(other):
        block = jnp.concatenate([w[k] for w in (wq, wk, wv)], 1)
        total = total + jnp.dot(piece[...], block, preferred_element_type=F32)
    head_dim = cosine.shape[1]
    c, s = cosine[...], sine[...]
    half = head_dim // 2
    turns = []
    for i, scale in enumerate((head_dim ** (-0.5), 1.0)):
        gain = gains[i : i + 1, :] * scale
        turns.append((c * gain, s * jnp.concatenate([gain[:, half:], gain[:, :half]], 1)))
    (q_cos, q_sin), (k_cos, k_sin) = turns

    def turned(raw, turn_cos, turn_sin):
        scale = lax.rsqrt(jnp.mean(raw * raw, -1, keepdims=True) + 1e-06)
        return (
            (raw * turn_cos + pltpu.roll(raw, half, 1) * turn_sin) * scale
        ).astype(BF16)

    heads = [total[:, h : h + head_dim] for h in range(0, total.shape[1], head_dim)]
    top = jnp.concatenate([turned(h, q_cos, q_sin) for h in heads[:-2]], 1)
    low = jnp.concatenate([turned(heads[-2], k_cos, k_sin), heads[-1].astype(BF16)], 1)
    first_half = lax.rem(iota(picks.shape[1:], 0), LINES) < SLOTS
    for g in range(PAIRS):
        picked, lines = picks[g], low
        if g == 0:
            zero = jnp.zeros_like(picked)
            parts = [jnp.where(first_half, picked, zero), jnp.where(first_half, zero, picked)]
            picked, lines = jnp.concatenate(parts, 1), jnp.concatenate([top, low], 0)
        held[g] = jnp.dot(picked, lines, preferred_element_type=F32).astype(BF16)
        to = out.at[:, g * width : (g + 1) * width]
        copies.append(pltpu.make_async_copy(held.at[g], to, sems.at[g]))
        copies[-1].start()
    for copy in copies:
        copy.wait()


def land_kernel(
    me_ref, arrived, queries, keyvalues, sent, key_docs, query_docs, doc_lines
):
    me = me_ref[0]
    rows = key_docs.shape[1]
    width = keyvalues.shape[1]
    head_dim = queries.shape[1]
    noted = arrived[:, PAIRS * width :].astype(F32)
    doc_lines[...] = noted
    labels = noted.T
    shape = labels.shape
    first = lax.rem(iota(shape, 1), LINES) < SLOTS
    spot = (iota(shape, 0) + 1).astype(F32)
    for g in range(PAIRS):
        lands = labels[g : g + 1, :] == spot
        landing = jnp.concatenate([hot(lands & first), hot(lands & ~first)], 0)
        placed = jnp.dot(
            landing, arrived[:, g * width : (g + 1) * width], preferred_element_type=F32
        ).astype(BF16)
        if g == 0:
            for h in range(queries.shape[0] // rows):
                queries[h * rows : (h + 1) * rows, :] = placed[
                    :rows, h * head_dim : (h + 1) * head_dim
                ]
            keyvalues[:rows, :] = placed[rows:, :]
        else:
            keyvalues[(2 * g - 1) * rows : (2 * g + 1) * rows, :] = placed
    begin = pl.multiple_of(lax.rem(me, 2) * rows, rows)
    sent[...] = keyvalues[pl.ds(begin, sent.shape[0]), :]
    for back in range(SPAN + 1):
        owner = pl.multiple_of(jnp.maximum(me - back, 0) * LINES, LINES)
        lines = doc_lines[pl.ds(owner, LINES), :]
        docs = jnp.concatenate([lines[h : h + 1, NOTED:] for h in range(rows // NOTED)], 1)
        key_docs[back : back + 1, :] = jnp.where(me >= back, docs.astype(I32), -1)
        if back == 0:
            own_docs = column(docs)
            for h in range(queries.shape[0] // rows):
                query_docs[h * rows : (h + 1) * rows, :] = own_docs.astype(I32)
    key_docs[SPAN + 1 :, :] = jnp.full((key_docs.shape[0] - SPAN - 1, rows), -1, I32)


def attend(backs, rows, queries, query_docs, key_docs, keyvalues):
    head_dim = queries.shape[1]
    q = queries[...]
    q_doc = query_docs[...]
    scores = lax.dot_general(
        q, keyvalues[:, :head_dim], (((1,), (1,)), ((), ())), preferred_element_type=F32
    )
    docs = jnp.concatenate([key_docs[back : back + 1, :] for back in backs], 1)
    visible = q_doc == docs
    if 0 in backs:
        t, u = lax.rem(iota(scores.shape, 0), rows), iota(scores.shape, 1)
        visible = visible & ((u <= t) | (u >= rows))
    weights = jnp.where(visible, jnp.exp(scores), 0.0)
    denom = jnp.sum(weights, 1, keepdims=True)
    numer = jnp.dot(weights.astype(BF16), keyvalues[:, head_dim:], preferred_element_type=F32)
    return numer, denom


def attend_first_kernel(backs, queries, query_docs, key_docs, keyvalues, numer, denom):
    rows = key_docs.shape[1]
    n, d = attend(backs, rows, queries, query_docs, key_docs, keyvalues)
    numer[...] = n
    denom[...] = jnp.broadcast_to(d, denom.shape)


def attend_last_kernel(backs, queries, query_docs, key_docs, keyvalues, numer, denom, out):
    rows = out.shape[0]
    head_dim = queries.shape[1]
    n, d = attend(backs, rows, queries, query_docs, key_docs, keyvalues)
    result = ((numer[...] + n) / (denom[...] + d)).astype(BF16)
    for h in range(out.shape[1] // head_dim):
        out[:, h * head_dim : (h + 1) * head_dim] = result[h * rows : (h + 1) * rows, :]


TABLES_COST = 2 * 10**10
VMEM = pl.BlockSpec(memory_space=pltpu.VMEM)
SMEM = pl.BlockSpec(memory_space=pltpu.SMEM)
HBM = pl.BlockSpec(memory_space=pltpu.HBM)


def call(kernel, outs, operands, away=(), scratch=(), limit=24, cost=None, out_spec=VMEM):
    shapes = [jax.ShapeDtypeStruct(s, t) for s, t in outs]
    return pl.pallas_call(
        kernel,
        out_shape=shapes,
        in_specs=[SMEM if x.shape == (1,) else VMEM for x in operands] + [HBM] * len(away),
        out_specs=[out_spec] * len(shapes),
        scratch_shapes=scratch,
        cost_estimate=cost and pl.CostEstimate(flops=cost, bytes_accessed=0, transcendentals=0),
        compiler_params=pltpu.CompilerParams(vmem_limit_bytes=limit * 2**20),
    )(*operands, *[pltpu.with_memory_space_constraint(x, pltpu.HBM) for x in away])


def rotation(positions, head_dim):
    half_dim = head_dim // 2
    exponent = jnp.arange(half_dim, dtype=F32) * (2.0 / head_dim)
    frequency = jnp.power(jnp.float32(1000000.0), -exponent)
    angles = positions.astype(F32)[:, None] * frequency[None, :]
    cosine, sine = jnp.cos(angles), jnp.sin(angles)
    return jnp.concatenate([cosine, cosine], 1), jnp.concatenate([-sine, sine], 1)


def body(hidden, destination, doc_ids, w_query, w_key, w_value, q_gain, k_gain):
    blocks = lax.axis_size("ctx")
    rows, width = hidden.shape
    q_width = w_query.shape[1]
    head_dim = q_gain.shape[0]
    q_rows = q_width // head_dim * rows
    me_kvh = lax.axis_index("kvh").astype(I32).reshape(1)
    me_ctx = lax.axis_index("ctx").astype(I32).reshape(1)

    n = lax.axis_size("kvh")
    along_x = [list(range(side, n, 2)) for side in range(2)]
    members = len(along_x[0])
    across = lax.ppermute(hidden, "kvh", [(i, i ^ 1) for i in range(n)])
    (spread,) = call(
        spread_own_kernel,
        [((members, rows, width), BF16)],
        [hidden],
    )
    mine = lax.all_to_all(spread, "kvh", 0, 0, tiled=True, axis_index_groups=along_x)
    cosine, sine = rotation(destination, head_dim)
    lines = blocks * LINES
    picks, notes, gains = call(
        tables_kernel,
        [((PAIRS, lines, rows), BF16), ((lines, rows), BF16), ((2, head_dim), F32)],
        [],
        [destination.reshape(1, -1), doc_ids.reshape(1, -1)]
        + [q_gain.reshape(1, -1), k_gain.reshape(1, -1)],
        scratch=[pltpu.VMEM((1, rows), I32)] * 2 + [pltpu.SemaphoreType.DMA((4,))],
        cost=TABLES_COST,
    )
    shifts = (0, 3, 2, 1)
    other = [across] + [
        lax.ppermute(across, "kvh", [(i, (i + 2 * d) % n) for i in range(n)]) for d in shifts[1:]
    ]

    columns = PAIRS * 2 * head_dim + rows
    weights = [w_query, w_key, w_value]
    all_heads = q_width + 2 * head_dim
    held = [((members, width, w.shape[1]), BF16) for w in weights]
    sems = pltpu.SemaphoreType.DMA((members, len(weights)))
    first, *ahead = call(
        functools.partial(project_first_kernel, shifts),
        [((rows, all_heads), F32), *held],
        [me_kvh, mine],
        weights,
        scratch=[pltpu.VMEM(*h) for h in held] + [sems, sems],
    )
    (parcel,) = call(
        project_kernel,
        [((lines, columns), BF16)],
        [first, cosine, sine, gains, picks, notes, *ahead, *other],
        scratch=[
            pltpu.VMEM((PAIRS, lines, 2 * head_dim), BF16),
            pltpu.SemaphoreType.DMA((PAIRS + 1,)),
        ],
        out_spec=HBM,
    )
    arrived = lax.all_to_all(
        parcel.reshape(blocks, LINES, columns), "ctx", split_axis=0, concat_axis=0, tiled=True
    ).reshape(lines, columns)
    held = SPAN // 2 + 1
    queries, keyvalues, sent, key_docs, query_docs = call(
        land_kernel,
        [
            ((q_rows, head_dim), BF16),
            ((held * rows, 2 * head_dim), BF16),
            (((held - 1) * rows, 2 * head_dim), BF16),
            ((16, rows), I32),
            ((q_rows, 1), I32),
        ],
        [me_ctx, arrived],
        scratch=[pltpu.VMEM((lines, rows), F32)],
    )

    swapped = lax.ppermute(sent, "ctx", [(i, i ^ 1) for i in range(blocks)])
    numer, denom = call(
        functools.partial(attend_first_kernel, tuple(range(0, SPAN + 1, 2))),
        [((q_rows, head_dim), F32)] * 2,
        [queries, query_docs, key_docs, keyvalues],
    )
    (out,) = call(
        functools.partial(attend_last_kernel, tuple(range(1, SPAN + 1, 2))),
        [((rows, q_width), BF16)],
        [queries, query_docs, key_docs, swapped, numer, denom],
    )
    return out


def solution(mesh):
    placed = (
        P("ctx", "kvh"),
        P("ctx"),
        P("ctx"),
        P(None, "kvh"),
        P(None, "kvh"),
        P(None, "kvh"),
        P(),
        P(),
    )
    return jax.shard_map(
        body, mesh=mesh, in_specs=placed, out_specs=P("ctx", "kvh"), check_vma=False
    )
```

```python
import functools

import jax
import jax.numpy as jnp
from jax import lax
from jax.experimental import pallas as pl
from jax.experimental.pallas import tpu as pltpu
from jax.sharding import PartitionSpec as P

SPAN = 8
SLOTS = 4
PARTS = 1 + SPAN // 2 + 1
PAIRS = PARTS // 2
LINES = 2 * SLOTS
NOTED = 64
F32, BF16, I32 = jnp.float32, jnp.bfloat16, jnp.int32


def block_back(part):
    return 2 * max(part - 1, 0)


def iota(shape, dim):
    return lax.broadcasted_iota(I32, shape, dim)


def hot(mask):
    return jnp.where(mask, 1.0, 0.0).astype(BF16)


def column(row):
    square = (row.shape[1], row.shape[1])
    return jnp.sum(jnp.where(iota(square, 0) == iota(square, 1), row, 0), 1, keepdims=True)


def fetch(pairs, sems):
    copies = [pltpu.make_async_copy(a, b, sems.at[i]) for i, (a, b) in enumerate(pairs)]
    for copy in copies:
        copy.start()
    for copy in copies:
        copy.wait()


def spread_own_kernel(hidden, spread):
    for i in range(spread.shape[0]):
        spread[i] = hidden[...]


def tables_kernel(
    destination, doc_ids, q_gain, k_gain, picks, notes, gains, place_ref, docs_ref, sems
):
    gain_rows = [(g, gains.at[i : i + 1]) for i, g in enumerate((q_gain, k_gain))]
    fetch([(destination, place_ref), (doc_ids, docs_ref)] + gain_rows, sems)
    place, docs = place_ref[...], docs_ref[...]
    rows = place.shape[1]
    target, inside = lax.div(place, rows), lax.rem(place, rows)
    square = (rows, rows)
    earlier = (column(target) == target) & (iota(square, 0) < iota(square, 1))
    order = jnp.sum(jnp.where(earlier, 1, 0), 0, keepdims=True)
    slot = (target * SLOTS + order).reshape(1, 1, rows)
    label = column(inside) + 1
    shape = (notes.shape[0] // LINES, LINES, rows)
    flat = notes.shape
    block, line = iota(shape, 0), iota(shape, 1)
    noted = jnp.zeros(flat, F32)
    for g in range(PAIRS):
        back = jnp.where(line < SLOTS, block_back(2 * g), block_back(2 * g + 1))
        at = jnp.where(line < SLOTS, line, line - SLOTS)
        found = (block - back) * SLOTS + at == slot
        picked = jnp.where(found, 1.0, 0.0).reshape(flat).astype(BF16)
        picks[g] = picked
        lane = jnp.where(iota(square, 1) == g, label, 0).astype(F32).astype(BF16)
        noted += jnp.dot(picked, lane, preferred_element_type=F32)
    kept = docs.astype(F32)
    halves = [jnp.concatenate([jnp.zeros((1, rows - NOTED), F32), kept[:, h : h + NOTED]], 1) for h in range(0, rows, NOTED)]
    doc_lines = sum(
        jnp.where(line == h, half.reshape(1, 1, rows), 0.0) for h, half in enumerate(halves)
    )
    notes[...] = (noted + doc_lines.reshape(flat)).astype(BF16)


def weight_copies(weights, held, sems, owners):
    width = held[0].shape[1]
    copies = []
    for k, owner in enumerate(owners):
        span = pl.ds(pl.multiple_of(owner * width, width), width)
        copies.append(
            [
                pltpu.make_async_copy(w.at[span, :], to.at[k], sems.at[k, i])
                for i, (w, to) in enumerate(zip(weights, held))
            ]
        )
        for copy in copies[-1]:
            copy.start()
    return copies


def project_first_kernel(shifts, me_ref, mine, wq, wk, wv, first, *refs):
    ahead, held, (sems, ahead_sems) = refs[:3], refs[3:6], refs[6:]
    side = lax.rem(me_ref[0], 2)
    owners = [2 * k + side for k in range(mine.shape[0])]
    steps = weight_copies((wq, wk, wv), held, sems, owners)
    groups = wq.shape[0] // held[0].shape[1]
    partner = me_ref[0] + 1 - 2 * side
    owners = [lax.rem(partner + groups - 2 * d, groups) for d in shifts]
    later = weight_copies((wq, wk, wv), ahead, ahead_sems, owners)
    total = 0.0
    for k, copies in enumerate(steps):
        for copy in copies:
            copy.wait()
        block = jnp.concatenate([to[k] for to in held], 1)
        total = total + jnp.dot(mine[k], block, preferred_element_type=F32)
    first[...] = total
    for copies in later:
        for copy in copies:
            copy.wait()


def project_kernel(
    first, cosine, sine, gains, picks, notes, wq, wk, wv, *refs
):
    other, (out, held, sems) = refs[:-3], refs[-3:]
    width = held.shape[2]
    kept = out.at[:, PAIRS * width :]
    copies = [pltpu.make_async_copy(notes, kept, sems.at[PAIRS])]
    copies[0].start()
    total = first[...]
    for k, piece in enumerate(other):
        block = jnp.concatenate([w[k] for w in (wq, wk, wv)], 1)
        total = total + jnp.dot(piece[...], block, preferred_element_type=F32)
    head_dim = cosine.shape[1]
    c, s = cosine[...], sine[...]
    half = head_dim // 2
    turns = []
    for i, scale in enumerate((head_dim ** (-0.5), 1.0)):
        gain = gains[i : i + 1, :] * scale
        turns.append((c * gain, s * jnp.concatenate([gain[:, half:], gain[:, :half]], 1)))
    (q_cos, q_sin), (k_cos, k_sin) = turns

    def turned(raw, turn_cos, turn_sin):
        scale = lax.rsqrt(jnp.mean(raw * raw, -1, keepdims=True) + 1e-06)
        return (
            (raw * turn_cos + pltpu.roll(raw, half, 1) * turn_sin) * scale
        ).astype(BF16)

    heads = [total[:, h : h + head_dim] for h in range(0, total.shape[1], head_dim)]
    top = jnp.concatenate([turned(h, q_cos, q_sin) for h in heads[:-2]], 1)
    low = jnp.concatenate([turned(heads[-2], k_cos, k_sin), heads[-1].astype(BF16)], 1)
    first_half = lax.rem(iota(picks.shape[1:], 0), LINES) < SLOTS
    for g in range(PAIRS):
        picked, lines = picks[g], low
        if g == 0:
            zero = jnp.zeros_like(picked)
            parts = [jnp.where(first_half, picked, zero), jnp.where(first_half, zero, picked)]
            picked, lines = jnp.concatenate(parts, 1), jnp.concatenate([top, low], 0)
        held[g] = jnp.dot(picked, lines, preferred_element_type=F32).astype(BF16)
        to = out.at[:, g * width : (g + 1) * width]
        copies.append(pltpu.make_async_copy(held.at[g], to, sems.at[g]))
        copies[-1].start()
    for copy in copies:
        copy.wait()


def land_kernel(
    me_ref, arrived, queries, keyvalues, sent, key_docs, query_docs, doc_lines
):
    me = me_ref[0]
    rows = key_docs.shape[1]
    width = keyvalues.shape[1]
    head_dim = queries.shape[1]
    noted = arrived[:, PAIRS * width :].astype(F32)
    doc_lines[...] = noted
    labels = noted.T
    shape = labels.shape
    first = lax.rem(iota(shape, 1), LINES) < SLOTS
    spot = (iota(shape, 0) + 1).astype(F32)
    for g in range(PAIRS):
        lands = labels[g : g + 1, :] == spot
        landing = jnp.concatenate([hot(lands & first), hot(lands & ~first)], 0)
        placed = jnp.dot(
            landing, arrived[:, g * width : (g + 1) * width], preferred_element_type=F32
        ).astype(BF16)
        if g == 0:
            for h in range(queries.shape[0] // rows):
                queries[h * rows : (h + 1) * rows, :] = placed[
                    :rows, h * head_dim : (h + 1) * head_dim
                ]
            keyvalues[:rows, :] = placed[rows:, :]
        else:
            keyvalues[(2 * g - 1) * rows : (2 * g + 1) * rows, :] = placed
    begin = pl.multiple_of(lax.rem(me, 2) * rows, rows)
    sent[...] = keyvalues[pl.ds(begin, sent.shape[0]), :]
    for back in range(SPAN + 1):
        owner = pl.multiple_of(jnp.maximum(me - back, 0) * LINES, LINES)
        lines = doc_lines[pl.ds(owner, LINES), :]
        docs = jnp.concatenate([lines[h : h + 1, NOTED:] for h in range(rows // NOTED)], 1)
        key_docs[back : back + 1, :] = jnp.where(me >= back, docs.astype(I32), -1)
        if back == 0:
            own_docs = column(docs)
            for h in range(queries.shape[0] // rows):
                query_docs[h * rows : (h + 1) * rows, :] = own_docs.astype(I32)
    key_docs[SPAN + 1 :, :] = jnp.full((key_docs.shape[0] - SPAN - 1, rows), -1, I32)


def attend(backs, rows, queries, query_docs, key_docs, keyvalues):
    head_dim = queries.shape[1]
    q = queries[...]
    q_doc = query_docs[...]
    scores = lax.dot_general(
        q, keyvalues[:, :head_dim], (((1,), (1,)), ((), ())), preferred_element_type=F32
    )
    docs = jnp.concatenate([key_docs[back : back + 1, :] for back in backs], 1)
    visible = q_doc == docs
    if 0 in backs:
        t, u = lax.rem(iota(scores.shape, 0), rows), iota(scores.shape, 1)
        visible = visible & ((u <= t) | (u >= rows))
    weights = jnp.where(visible, jnp.exp(scores), 0.0)
    denom = jnp.sum(weights, 1, keepdims=True)
    numer = jnp.dot(weights.astype(BF16), keyvalues[:, head_dim:], preferred_element_type=F32)
    return numer, denom


def attend_first_kernel(backs, queries, query_docs, key_docs, keyvalues, numer, denom):
    rows = key_docs.shape[1]
    n, d = attend(backs, rows, queries, query_docs, key_docs, keyvalues)
    numer[...] = n
    denom[...] = jnp.broadcast_to(d, denom.shape)


def attend_last_kernel(backs, queries, query_docs, key_docs, keyvalues, numer, denom, out):
    rows = out.shape[0]
    head_dim = queries.shape[1]
    n, d = attend(backs, rows, queries, query_docs, key_docs, keyvalues)
    result = ((numer[...] + n) / (denom[...] + d)).astype(BF16)
    for h in range(out.shape[1] // head_dim):
        out[:, h * head_dim : (h + 1) * head_dim] = result[h * rows : (h + 1) * rows, :]


TABLES_COST = 2 * 10**10
VMEM = pl.BlockSpec(memory_space=pltpu.VMEM)
SMEM = pl.BlockSpec(memory_space=pltpu.SMEM)
HBM = pl.BlockSpec(memory_space=pltpu.HBM)


def call(kernel, outs, operands, away=(), scratch=(), limit=24, cost=None, out_spec=VMEM):
    shapes = [jax.ShapeDtypeStruct(s, t) for s, t in outs]
    return pl.pallas_call(
        kernel,
        out_shape=shapes,
        in_specs=[SMEM if x.shape == (1,) else VMEM for x in operands] + [HBM] * len(away),
        out_specs=[out_spec] * len(shapes),
        scratch_shapes=scratch,
        cost_estimate=cost and pl.CostEstimate(flops=cost, bytes_accessed=0, transcendentals=0),
        compiler_params=pltpu.CompilerParams(vmem_limit_bytes=limit * 2**20),
    )(*operands, *[pltpu.with_memory_space_constraint(x, pltpu.HBM) for x in away])


def rotation(positions, head_dim):
    half_dim = head_dim // 2
    exponent = jnp.arange(half_dim, dtype=F32) * (2.0 / head_dim)
    frequency = jnp.power(jnp.float32(1000000.0), -exponent)
    angles = positions.astype(F32)[:, None] * frequency[None, :]
    cosine, sine = jnp.cos(angles), jnp.sin(angles)
    return jnp.concatenate([cosine, cosine], 1), jnp.concatenate([-sine, sine], 1)


def body(hidden, destination, doc_ids, w_query, w_key, w_value, q_gain, k_gain):
    blocks = lax.axis_size("ctx")
    rows, width = hidden.shape
    q_width = w_query.shape[1]
    head_dim = q_gain.shape[0]
    q_rows = q_width // head_dim * rows
    me_kvh = lax.axis_index("kvh").astype(I32).reshape(1)
    me_ctx = lax.axis_index("ctx").astype(I32).reshape(1)

    n = lax.axis_size("kvh")
    along_x = [list(range(side, n, 2)) for side in range(2)]
    members = len(along_x[0])
    across = lax.ppermute(hidden, "kvh", [(i, i ^ 1) for i in range(n)])
    (spread,) = call(
        spread_own_kernel,
        [((members, rows, width), BF16)],
        [hidden],
    )
    mine = lax.all_to_all(spread, "kvh", 0, 0, tiled=True, axis_index_groups=along_x)
    cosine, sine = rotation(destination, head_dim)
    lines = blocks * LINES
    picks, notes, gains = call(
        tables_kernel,
        [((PAIRS, lines, rows), BF16), ((lines, rows), BF16), ((2, head_dim), F32)],
        [],
        [destination.reshape(1, -1), doc_ids.reshape(1, -1)]
        + [q_gain.reshape(1, -1), k_gain.reshape(1, -1)],
        scratch=[pltpu.VMEM((1, rows), I32)] * 2 + [pltpu.SemaphoreType.DMA((4,))],
        cost=TABLES_COST,
    )
    shifts = (0, 2, 1, 3)
    other = [across] + [
        lax.ppermute(across, "kvh", [(i, (i + 2 * d) % n) for i in range(n)]) for d in shifts[1:]
    ]

    columns = PAIRS * 2 * head_dim + rows
    weights = [w_query, w_key, w_value]
    all_heads = q_width + 2 * head_dim
    held = [((members, width, w.shape[1]), BF16) for w in weights]
    sems = pltpu.SemaphoreType.DMA((members, len(weights)))
    first, *ahead = call(
        functools.partial(project_first_kernel, shifts),
        [((rows, all_heads), F32), *held],
        [me_kvh, mine],
        weights,
        scratch=[pltpu.VMEM(*h) for h in held] + [sems, sems],
    )
    (parcel,) = call(
        project_kernel,
        [((lines, columns), BF16)],
        [first, cosine, sine, gains, picks, notes, *ahead, *other],
        scratch=[
            pltpu.VMEM((PAIRS, lines, 2 * head_dim), BF16),
            pltpu.SemaphoreType.DMA((PAIRS + 1,)),
        ],
        out_spec=HBM,
    )
    arrived = lax.all_to_all(
        parcel.reshape(blocks, LINES, columns), "ctx", split_axis=0, concat_axis=0, tiled=True
    ).reshape(lines, columns)
    held = SPAN // 2 + 1
    queries, keyvalues, sent, key_docs, query_docs = call(
        land_kernel,
        [
            ((q_rows, head_dim), BF16),
            ((held * rows, 2 * head_dim), BF16),
            (((held - 1) * rows, 2 * head_dim), BF16),
            ((16, rows), I32),
            ((q_rows, 1), I32),
        ],
        [me_ctx, arrived],
        scratch=[pltpu.VMEM((lines, rows), F32)],
    )

    swapped = lax.ppermute(sent, "ctx", [(i, i ^ 1) for i in range(blocks)])
    numer, denom = call(
        functools.partial(attend_first_kernel, tuple(range(0, SPAN + 1, 2))),
        [((q_rows, head_dim), F32)] * 2,
        [queries, query_docs, key_docs, keyvalues],
    )
    (out,) = call(
        functools.partial(attend_last_kernel, tuple(range(1, SPAN + 1, 2))),
        [((rows, q_width), BF16)],
        [queries, query_docs, key_docs, swapped, numer, denom],
    )
    return out


def solution(mesh):
    placed = (
        P("ctx", "kvh"),
        P("ctx"),
        P("ctx"),
        P(None, "kvh"),
        P(None, "kvh"),
        P(None, "kvh"),
        P(),
        P(),
    )
    return jax.shard_map(
        body, mesh=mesh, in_specs=placed, out_specs=P("ctx", "kvh"), check_vma=False
    )
```
